32 devices in a mesh: row: 16 (over z, x, core), col: 2 (over y).
Axes of the slice: x: 2, y: 2, z: 4, core: 2. Of those that a mesh axis runs over, the one named last changes fastest.
Arguments:
- start_vectors: float32 [16384, 256], P('row', 'col'), may hold values from -6 to 6
- ham_blocks: float32 [128, 8, 128, 128], P(('row', 'col')), may hold values from -0.1875 to 0.1875
- block_cols: int32 [128, 8], P(('row', 'col')), may hold values from 0 to 127, as said below
- block_counts: int32 [128], P(('row', 'col')), may hold values from 1 to 8, as said below
- check_weights: float32 [256], replicated, may hold values from -0.375 to 0.375
Outputs:
- filtered: float32 [16384, 256], P('row', 'col')
- checksum: float32 [16384], P(('row', 'col'))
The draws below stay inside these ranges and needn't reach their ends.
Inputs may be any that keep to these rules, and one draw needn't show every extreme that they name: `block_cols`: slot j of block row b names block column (b + d) mod 128 for offsets d that are distinct within the row and lie from -4 to 3; slot 0 names the block row itself (d = 0). Only the first block_counts[b] slots of block row b are part of the operator. The block rows of one thirty-second of the devices (at least one device) hold 8 live slots each, all block rows of such a device alike; every other block row holds 1 to 3.
All inputs are finite; a program needn't handle non-finite values.
Results may differ from the reference program's by a relative error of at most 0.0003.
Values sent between devices are 32-bit elements; how exact they have to be, the bound alone decides.
A program may use at most 64 MiB of HBM per device.

```python
import jax
import jax.numpy as jnp
from jax import lax

B = 128
K = 256
BRD = 4
REACH = 4
ITERS = 3
CAP = 8
NBR = 128
N = 16384


def block_pattern(key):
    device_count = NBR // BRD
    heavy_number = max(1, device_count // 32)
    device_order = jax.random.permutation(jax.random.fold_in(key, 101), device_count)
    heavy_devices = jnp.zeros((device_count,), jnp.int32).at[device_order[:heavy_number]].set(1)
    heavy_rows = jnp.repeat(heavy_devices, BRD)
    light_counts = jax.random.randint(jax.random.fold_in(key, 102), (NBR,), 1, 4)
    counts = jnp.where(heavy_rows > 0, CAP, light_counts).astype(jnp.int32)
    random_scores = jax.random.randint(jax.random.fold_in(key, 103), (NBR, CAP), 0, 1 << 20)
    scores = random_scores * CAP + jnp.arange(CAP, dtype=jnp.int32)[None, :]
    scores = scores.at[:, REACH].set(-1)
    chosen = jnp.argsort(scores, axis=1).astype(jnp.int32)
    offsets = chosen - REACH
    columns = jnp.mod(jnp.arange(NBR, dtype=jnp.int32)[:, None] + offsets, NBR).astype(jnp.int32)
    return (columns, counts)


def draw_block_cols(key, part):
    columns, counts = block_pattern(jax.random.fold_in(key, 7))
    return columns


def draw_block_counts(key, part):
    columns, counts = block_pattern(jax.random.fold_in(key, 7))
    return counts


def levels(stream_key, shape, split, smallest, high):
    def one(axis_at, blocks):
        heights = jax.random.uniform(jax.random.fold_in(jax.random.fold_in(stream_key, 6), axis_at), (blocks,), jnp.float32, smallest / len(split), high / len(split))
        return jnp.repeat(jnp.exp(heights), shape[axis_at] // blocks).reshape((-1,) + (1,) * (len(shape) - axis_at - 1))

    level = one(*split[0])
    for cut in split[1:]:
        level = level * one(*cut)
    return level


def scatter_about(stream_key, dims, deviation, reach, cuts=(), held_as=jnp.bfloat16):
    result = deviation * jax.random.normal(stream_key, dims, jnp.float32)
    if cuts:
        result = result * levels(stream_key, dims, cuts, -0.22, 0.18)
    return jnp.clip(result, -reach, reach).astype(held_as)


def setup_inputs(seed: int = 0) -> dict:
    streams_of = jax.random.split(jax.random.key(seed), 6)
    start_vectors = scatter_about(streams_of[0], (N, K), 1.0, 6.0, ((0, 16), (1, 2)), jnp.float32)
    ham_blocks = scatter_about(streams_of[1], (NBR, CAP, B, B), (B * CAP) ** -0.5, 0.1875, ((0, 32),), jnp.float32)
    block_cols = draw_block_cols(jax.random.fold_in(streams_of[5], 71), 0)
    block_counts = draw_block_counts(jax.random.fold_in(streams_of[5], 71), 0)
    check_weights = scatter_about(streams_of[4], (K,), K ** -0.5, 0.375, (), jnp.float32)
    return {"start_vectors": start_vectors, "ham_blocks": ham_blocks, "block_cols": block_cols, "block_counts": block_counts, "check_weights": check_weights}


CENTRE = 0.25
HALF_WIDTH = 1.5


def apply_operator(ham_blocks, block_cols, block_counts, vectors, checks):
    block_size = ham_blocks.shape[2]
    slot_count = ham_blocks.shape[1]
    vector_tiles = vectors.reshape(-1, block_size, vectors.shape[1])
    check_tiles = checks.reshape(-1, block_size)

    def one_row(inputs):
        matrices, columns, live_count = inputs
        live_mask = (jnp.arange(slot_count, dtype=jnp.int32) < live_count).astype(matrices.dtype)
        masked = matrices * live_mask[:, None, None]
        gathered = vector_tiles[columns]
        gathered_check = check_tiles[columns]
        product = jnp.einsum("jab,jbk->ak", masked, gathered, precision=lax.Precision.HIGHEST)
        product_check = jnp.einsum("jab,jb->a", masked, gathered_check, precision=lax.Precision.HIGHEST)
        return product, product_check

    products, product_checks = lax.map(one_row, (ham_blocks, block_cols, block_counts))
    return products.reshape(vectors.shape), product_checks.reshape(checks.shape)


def reference(start_vectors, ham_blocks, block_cols, block_counts, check_weights):
    checks = jnp.dot(start_vectors, check_weights, precision=lax.Precision.HIGHEST, preferred_element_type=jnp.float32)
    previous, previous_check = start_vectors, checks
    image_rows, image_check = apply_operator(ham_blocks, block_cols, block_counts, start_vectors, checks)
    current = (image_rows - CENTRE * start_vectors) / HALF_WIDTH
    current_check = (image_check - CENTRE * checks) / HALF_WIDTH
    for step_index in range(ITERS - 1):
        image_rows, image_check = apply_operator(ham_blocks, block_cols, block_counts, current, current_check)
        following = 2.0 * (image_rows - CENTRE * current) / HALF_WIDTH - previous
        following_check = 2.0 * (image_check - CENTRE * current_check) / HALF_WIDTH - previous_check
        previous, previous_check = current, current_check
        current, current_check = following, following_check
    return current, current_check
```

```python
import functools

import jax
import jax.numpy as jnp
from jax import lax
from jax.experimental import pallas as pl
from jax.experimental.pallas import tpu as pltpu
from jax.sharding import PartitionSpec as P

REACH = 4
RIGHT_REACH = 3
LIGHT = 3
ITERS = 3


CENTRE = 0.25
HALF_WIDTH = 1.5
HIGHEST_PRECISION = lax.Precision.HIGHEST
MESH = pl.DeviceIdType.MESH


def shifted_2(value, axis, steps):
    count = lax.axis_size(axis)
    pairs = [(source, (source + steps) % count) for source in range(count)]
    return lax.ppermute(value, axis, pairs)


def accumulate(ham_blocks, block_cols, finishes, window, window_check, base_block, total_blocks):
    block_size = ham_blocks.shape[2]
    vector_width = window.shape[1]
    results = []
    result_checks = []
    for row_index in range(ham_blocks.shape[0]):
        matrices = ham_blocks[row_index]
        columns = block_cols[row_index]

        def add_block(slot_index, carried, matrices=matrices, columns=columns):
            summed, summed_check = carried
            offset = jnp.mod(columns[slot_index] - base_block, total_blocks) * block_size
            segment = lax.dynamic_slice_in_dim(window, offset, block_size, 0)
            segment_check = lax.dynamic_slice_in_dim(window_check, offset, block_size, 0)
            matrix = lax.dynamic_index_in_dim(matrices, slot_index, 0, keepdims=False)
            summed = summed + jnp.dot(
                matrix, segment, precision=HIGHEST_PRECISION, preferred_element_type=jnp.float32
            )
            summed_check = summed_check + jnp.dot(
                matrix,
                segment_check,
                precision=HIGHEST_PRECISION,
                preferred_element_type=jnp.float32,
            )
            return (summed, summed_check)

        initial = (
            jnp.zeros((block_size, vector_width), jnp.float32),
            jnp.zeros((block_size,), jnp.float32),
        )
        summed, summed_check = lax.fori_loop(0, finishes[row_index], add_block, initial)
        results.append(summed)
        result_checks.append(summed_check)
    return (jnp.concatenate(results, 0), jnp.concatenate(result_checks, 0))


def near_window(vectors, checks, reach_devices):
    pieces = []
    piece_checks = []
    for distance in range(-reach_devices, reach_devices + 1):
        if distance == 0:
            pieces.append(vectors)
            piece_checks.append(checks)
        else:
            shifted, shifted_check = shifted_2((vectors, checks), ("row", "col"), -distance)
            pieces.append(shifted)
            piece_checks.append(shifted_check)
    return (jnp.concatenate(pieces, 0), jnp.concatenate(piece_checks, 0))


def rows_split(start_vectors, ham_blocks, block_cols, block_counts, check_weights):
    row_vectors = lax.all_to_all(start_vectors, "col", split_axis=0, concat_axis=1, tiled=True)
    checks = jnp.dot(
        row_vectors, check_weights, precision=HIGHEST_PRECISION, preferred_element_type=jnp.float32
    )
    blocks_here = ham_blocks.shape[0]
    total_blocks = lax.axis_size(("row", "col")) * blocks_here
    position = lax.axis_index(("row", "col"))
    neighbours = (REACH + blocks_here - 1) // blocks_here
    base_block = (position - neighbours) * blocks_here

    def apply_operator(vectors, vector_checks):
        window, window_check = near_window(vectors, vector_checks, neighbours)
        return accumulate(
            ham_blocks, block_cols, block_counts, window, window_check, base_block, total_blocks
        )

    previous, previous_check = (row_vectors, checks)
    image_rows, image_check = apply_operator(row_vectors, checks)
    current = (image_rows - CENTRE * row_vectors) / HALF_WIDTH
    current_check = (image_check - CENTRE * checks) / HALF_WIDTH
    for step_index in range(ITERS - 1):
        image_rows, image_check = apply_operator(current, current_check)
        following = 2.0 * (image_rows - CENTRE * current) / HALF_WIDTH - previous
        following_check = 2.0 * (image_check - CENTRE * current_check) / HALF_WIDTH - previous_check
        previous, previous_check = (current, current_check)
        current, current_check = (following, following_check)
    filtered = lax.all_to_all(current, "col", split_axis=1, concat_axis=0, tiled=True)
    return (filtered, current_check)


def split2(x):
    high = x.astype(jnp.bfloat16)
    low = (x - high.astype(jnp.float32)).astype(jnp.bfloat16)
    return high, low


def beyond(count, slot):
    return jnp.minimum(jnp.maximum(count - slot, 0), 1)


def filter_kernel(
    rows_n, v_ref, h_ref, tab_ref, tabh_ref, w_ref, out_ref, chk_ref,
    hv, hr, es, em, er, tabv, tabp, a_ref, ea_ref, win, p_ref, y1, y2, halo, cs_s, cs_r,
    send, recv, loc,
):
    r = lax.axis_index("row")
    y = lax.axis_index("col")
    right, left = lax.rem(r + 1, rows_n), lax.rem(r + rows_n - 1, rows_n)
    core = lax.rem(r, 2)
    sib = r + 1 - 2 * core
    blocks, cap, size, _ = hv.shape
    group = 2 * blocks
    total = rows_n * group
    heavy_slots = cap - LIGHT
    half_rows = blocks // 2

    barrier = pltpu.get_barrier_semaphore()
    for target in ({"row": left}, {"row": right}, {"col": 1 - y}):
        pl.semaphore_signal(barrier, inc=1, device_id=target, device_id_type=MESH)

    own_copy = pltpu.make_async_copy(h_ref, hv, loc.at[0])
    own_copy.start()
    pl.semaphore_wait(barrier, 3)

    def remote(src, dst, index, target):
        return pltpu.make_async_remote_copy(
            src_ref=src, dst_ref=dst, send_sem=send.at[index], recv_sem=recv.at[index],
            device_id=target, device_id_type=MESH,
        )

    peer = {"col": 1 - y}
    sibling = {"row": sib}
    tab_copy = remote(tabh_ref, tabv, 0, peer)
    light_copy = remote(h_ref.at[:, pl.ds(0, LIGHT)], hr, 1, peer)
    merge_copy = remote(
        h_ref.at[pl.ds(half_rows * (1 - core), half_rows), pl.ds(LIGHT, heavy_slots)], es, 2, sibling
    )
    mine = pl.ds(half_rows * core, half_rows)
    cross_copy = remote(em, er.at[mine], 3, peer)
    share_copy = remote(er.at[mine], er.at[mine], 4, sibling)
    check_copy = remote(cs_s, cs_r, 5, peer)

    def halo_copies(source, step):
        own_rows = group * size
        to_right = remote(
            source.at[pl.ds(own_rows - REACH * size, REACH * size)],
            halo.at[step, pl.ds(0, REACH * size)], 6 + 2 * step, {"row": right},
        )
        to_left = remote(
            source.at[pl.ds(0, RIGHT_REACH * size)],
            halo.at[step, pl.ds(REACH * size, RIGHT_REACH * size)], 7 + 2 * step, {"row": left},
        )
        return to_right, to_left

    tab_copy.start()
    merge_copy.start()
    light_copy.start()
    first = halo_copies(v_ref, 0)
    first[0].start()
    first[1].start()

    def put_window(source, src_at, dst_at, count):
        def one(i, _):
            at = pl.multiple_of(src_at + i * size, size)
            high, low = split2(source[pl.ds(at, size), :])
            win[dst_at + i, :, pl.ds(0, size)] = high
            win[dst_at + i, :, pl.ds(size, size)] = low
            return 0

        lax.fori_loop(0, count, one, 0)

    def put_halo(step):
        put_window(halo.at[step], 0, 0, REACH)
        put_window(halo.at[step], REACH * size, REACH + group, RIGHT_REACH)

    def scalar(i, j):
        return tab_ref[i, j], tabp[i, j]

    own_is_heavy = beyond(tab_ref[0, cap], LIGHT)
    own_heavy = own_is_heavy.astype(jnp.float32)

    own_copy.wait()
    merge_copy.wait_recv()

    def merge(i, _):
        a = hv[half_rows * core + i, pl.ds(LIGHT, heavy_slots)]
        em[i] = a * own_heavy + es[i] * (1.0 - own_heavy)
        return 0

    lax.fori_loop(0, half_rows, merge, 0)
    cross_copy.start()

    def put_light(source, table, half):
        def one(i, _):
            count = table[i, cap]
            for j in range(LIGHT):
                live = beyond(count, j).astype(jnp.float32)
                high, low = split2(source[i, j] * live)
                a_ref[half * blocks + i, pl.ds(0, size), pl.ds(j * size, size)] = high
                a_ref[half * blocks + i, pl.ds(size, size), pl.ds(j * size, size)] = low
            return 0

        lax.fori_loop(0, blocks, one, 0)

    put_light(hv, tab_ref, y)
    put_window(v_ref, 0, REACH, group)

    tab_copy.wait_recv()
    tab_local = pltpu.make_async_copy(tabv, tabp, loc.at[1])
    tab_local.start()
    tab_local.wait()
    peer_heavy = beyond(tabp[0, cap], LIGHT).astype(jnp.float32)

    first[0].wait_recv()
    first[1].wait_recv()
    put_halo(0)

    light_copy.wait_recv()
    put_light(hr, tabp, 1 - y)

    cross_copy.wait_recv()
    share_copy.start()
    share_copy.wait_recv()

    def put_heavy(i, _):
        own_count, peer_count = scalar(i, cap)
        for j in range(heavy_slots):
            own_live = beyond(own_count, LIGHT + j).astype(jnp.float32)
            peer_live = beyond(peer_count, LIGHT + j).astype(jnp.float32) * (1.0 - own_heavy)
            high, low = split2(hv[i, LIGHT + j] * own_live + er[i, j] * peer_live)
            ea_ref[i, pl.ds(0, size), pl.ds(j * size, size)] = high
            ea_ref[i, pl.ds(size, size), pl.ds(j * size, size)] = low
        return 0

    lax.fori_loop(0, blocks, put_heavy, 0)

    base = r * group - REACH + total

    def tile(col):
        return win[jnp.minimum(lax.rem(col - base + 2 * total, total), win.shape[0] - 1)]

    def product(matrix, cols):
        tiles = jnp.concatenate([tile(col) for col in cols], 0)
        full = jnp.dot(matrix, tiles, preferred_element_type=jnp.float32)
        big = full[:size, :size]
        small = full[:size, size:] + full[size:, :size] + full[size:, size:]
        return big + small

    def heavy_products():
        def one(i, _):
            cols = []
            for j in range(heavy_slots):
                own_col, peer_col = scalar(i, LIGHT + j)
                cols.append(peer_col + own_is_heavy * (own_col - peer_col))
            p_ref[i] = product(ea_ref[i], cols)
            return 0

        lax.fori_loop(0, blocks, one, 0)

    def rows(half, source, older, target):
        mine = y * half + (1 - y) * (1 - half)
        share = mine.astype(jnp.float32)
        flag = own_heavy * share + peer_heavy * (1.0 - share)

        def one(i, _):
            cols = []
            for j in range(LIGHT):
                own_col, peer_col = scalar(i, j)
                cols.append(peer_col + mine * (own_col - peer_col))
            image = product(a_ref[half * blocks + i], cols) + p_ref[i] * flag
            at = pl.ds(pl.multiple_of((half * blocks + i) * size, size), size)
            value = (image - CENTRE * source[at, :]) * (1.0 / HALF_WIDTH)
            if older is not None:
                value = 2.0 * value - older[at, :]
            target[at, :] = value
            return 0

        lax.fori_loop(0, blocks, one, 0)

    chain = ((v_ref, None, y1), (y1, v_ref, y2), (y2, y1, out_ref))
    started = [*first]
    for step in range(ITERS):
        source, older, target = chain[step]
        if step:
            put_window(source, 0, REACH, group)
            started[2 * step].wait_recv()
            started[2 * step + 1].wait_recv()
            put_halo(step)
        heavy_products()
        if step < ITERS - 1:
            following = halo_copies(target, step + 1)
            started += following
            rows(1, source, older, target)
            following[0].start()
            rows(0, source, older, target)
            following[1].start()
        else:
            rows(1, source, older, target)
            rows(0, source, older, target)

    weights = jnp.where(y == 0, w_ref[:, :size], w_ref[:, size:])

    def partial(half):
        at = pl.ds(pl.multiple_of(half * blocks * size, size), blocks * size)
        return lax.dot_general(
            weights, out_ref[at, :], (((1,), (1,)), ((), ())),
            precision=HIGHEST_PRECISION, preferred_element_type=jnp.float32,
        )

    cs_s[...] = partial(1 - y)
    check_copy.start()
    own_part = partial(y)
    check_copy.wait_recv()
    chk_ref[...] = own_part + cs_r[...]

    for copy in (tab_copy, light_copy, merge_copy, cross_copy, share_copy, check_copy, *started):
        copy.wait_send()


def columns_split(start_vectors, ham_blocks, block_cols, block_counts, check_weights):
    blocks, cap, size, _ = ham_blocks.shape
    rows_n = lax.axis_size("row")
    group = 2 * blocks
    height, width = start_vectors.shape
    table = jnp.concatenate([block_cols, block_counts[:, None]], 1)
    table = jnp.pad(table, ((0, 8 - blocks), (0, 128 - cap - 1)))
    window = REACH + group + RIGHT_REACH
    f32, bf16 = jnp.float32, jnp.bfloat16
    heavy = cap - LIGHT
    vmem = pl.BlockSpec(memory_space=pltpu.VMEM)
    anywhere = pl.BlockSpec(memory_space=pl.ANY)
    filtered, check = pl.pallas_call(
        functools.partial(filter_kernel, rows_n),
        out_shape=(
            jax.ShapeDtypeStruct((height, width), f32),
            jax.ShapeDtypeStruct((1, blocks * size), f32),
        ),
        in_specs=[vmem, anywhere, pl.BlockSpec(memory_space=pltpu.SMEM), anywhere, vmem],
        out_specs=(vmem, vmem),
        scratch_shapes=[
            pltpu.VMEM((blocks, cap, size, size), f32),
            pltpu.VMEM((blocks, LIGHT, size, size), f32),
            pltpu.VMEM((blocks // 2, heavy, size, size), f32),
            pltpu.VMEM((blocks // 2, heavy, size, size), f32),
            pltpu.VMEM((blocks, heavy, size, size), f32),
            pltpu.VMEM((8, 128), jnp.int32),
            pltpu.SMEM((8, 128), jnp.int32),
            pltpu.VMEM((group, 2 * size, LIGHT * size), bf16),
            pltpu.VMEM((blocks, 2 * size, heavy * size), bf16),
            pltpu.VMEM((window, size, 2 * width), bf16),
            pltpu.VMEM((blocks, size, width), f32),
            pltpu.VMEM((height, width), f32),
            pltpu.VMEM((height, width), f32),
            pltpu.VMEM((ITERS, (REACH + RIGHT_REACH) * size, width), f32),
            pltpu.VMEM((1, blocks * size), f32),
            pltpu.VMEM((1, blocks * size), f32),
            pltpu.SemaphoreType.DMA((6 + 2 * ITERS,)),
            pltpu.SemaphoreType.DMA((6 + 2 * ITERS,)),
            pltpu.SemaphoreType.DMA((2,)),
        ],
        compiler_params=pltpu.CompilerParams(
            collective_id=0, has_side_effects=True, vmem_limit_bytes=40 * 1024 * 1024
        ),
    )(start_vectors, ham_blocks, table, table, check_weights.reshape(1, -1))
    return (filtered, check.reshape(-1))


def solution(mesh):
    placed = (
        P("row", "col"),
        P(("row", "col"), None, None, None),
        P(("row", "col"), None),
        P(("row", "col")),
        P(),
    )
    devices = mesh.shape["row"] * mesh.shape["col"]
    one_heavy = devices < 64 and mesh.shape["col"] == 2 and mesh.shape["row"] >= 4 and mesh.shape["row"] % 2 == 0
    return jax.shard_map(
        columns_split if one_heavy else rows_split,
        mesh=mesh,
        in_specs=placed,
        out_specs=(P("row", "col"), P(("row", "col"))),
        check_vma=False,
    )
```

```python
import functools

import jax
import jax.numpy as jnp
from jax import lax
from jax.experimental import pallas as pl
from jax.experimental.pallas import tpu as pltpu
from jax.sharding import PartitionSpec as P

REACH = 4
RIGHT_REACH = 3
LIGHT = 3
ITERS = 3


CENTRE = 0.25
HALF_WIDTH = 1.5
HIGHEST_PRECISION = lax.Precision.HIGHEST
MESH = pl.DeviceIdType.MESH


def shifted_2(value, axis, steps):
    count = lax.axis_size(axis)
    pairs = [(source, (source + steps) % count) for source in range(count)]
    return lax.ppermute(value, axis, pairs)


def accumulate(ham_blocks, block_cols, finishes, window, window_check, base_block, total_blocks):
    block_size = ham_blocks.shape[2]
    vector_width = window.shape[1]
    results = []
    result_checks = []
    for row_index in range(ham_blocks.shape[0]):
        matrices = ham_blocks[row_index]
        columns = block_cols[row_index]

        def add_block(slot_index, carried, matrices=matrices, columns=columns):
            summed, summed_check = carried
            offset = jnp.mod(columns[slot_index] - base_block, total_blocks) * block_size
            segment = lax.dynamic_slice_in_dim(window, offset, block_size, 0)
            segment_check = lax.dynamic_slice_in_dim(window_check, offset, block_size, 0)
            matrix = lax.dynamic_index_in_dim(matrices, slot_index, 0, keepdims=False)
            summed = summed + jnp.dot(
                matrix, segment, precision=HIGHEST_PRECISION, preferred_element_type=jnp.float32
            )
            summed_check = summed_check + jnp.dot(
                matrix,
                segment_check,
                precision=HIGHEST_PRECISION,
                preferred_element_type=jnp.float32,
            )
            return (summed, summed_check)

        initial = (
            jnp.zeros((block_size, vector_width), jnp.float32),
            jnp.zeros((block_size,), jnp.float32),
        )
        summed, summed_check = lax.fori_loop(0, finishes[row_index], add_block, initial)
        results.append(summed)
        result_checks.append(summed_check)
    return (jnp.concatenate(results, 0), jnp.concatenate(result_checks, 0))


def near_window(vectors, checks, reach_devices):
    pieces = []
    piece_checks = []
    for distance in range(-reach_devices, reach_devices + 1):
        if distance == 0:
            pieces.append(vectors)
            piece_checks.append(checks)
        else:
            shifted, shifted_check = shifted_2((vectors, checks), ("row", "col"), -distance)
            pieces.append(shifted)
            piece_checks.append(shifted_check)
    return (jnp.concatenate(pieces, 0), jnp.concatenate(piece_checks, 0))


def rows_split(start_vectors, ham_blocks, block_cols, block_counts, check_weights):
    row_vectors = lax.all_to_all(start_vectors, "col", split_axis=0, concat_axis=1, tiled=True)
    checks = jnp.dot(
        row_vectors, check_weights, precision=HIGHEST_PRECISION, preferred_element_type=jnp.float32
    )
    blocks_here = ham_blocks.shape[0]
    total_blocks = lax.axis_size(("row", "col")) * blocks_here
    position = lax.axis_index(("row", "col"))
    neighbours = (REACH + blocks_here - 1) // blocks_here
    base_block = (position - neighbours) * blocks_here

    def apply_operator(vectors, vector_checks):
        window, window_check = near_window(vectors, vector_checks, neighbours)
        return accumulate(
            ham_blocks, block_cols, block_counts, window, window_check, base_block, total_blocks
        )

    previous, previous_check = (row_vectors, checks)
    image_rows, image_check = apply_operator(row_vectors, checks)
    current = (image_rows - CENTRE * row_vectors) / HALF_WIDTH
    current_check = (image_check - CENTRE * checks) / HALF_WIDTH
    for step_index in range(ITERS - 1):
        image_rows, image_check = apply_operator(current, current_check)
        following = 2.0 * (image_rows - CENTRE * current) / HALF_WIDTH - previous
        following_check = 2.0 * (image_check - CENTRE * current_check) / HALF_WIDTH - previous_check
        previous, previous_check = (current, current_check)
        current, current_check = (following, following_check)
    filtered = lax.all_to_all(current, "col", split_axis=1, concat_axis=0, tiled=True)
    return (filtered, current_check)


def split2(x):
    high = x.astype(jnp.bfloat16)
    low = (x - high.astype(jnp.float32)).astype(jnp.bfloat16)
    return high, low


def beyond(count, slot):
    return jnp.minimum(jnp.maximum(count - slot, 0), 1)


def filter_kernel(
    rows_n, v_hbm, h_ref, cols_ref, counts_ref, colsh_ref, countsh_ref, w_hbm, out_ref, chk_ref,
    v_ref, w_ref, hv, hr, es, em, er, colsp, countsp, a_ref, ea_ref, win, p_ref, y1, y2, halo, cs_s, cs_r,
    send, recv, loc,
):
    r = lax.axis_index("row")
    y = lax.axis_index("col")
    right, left = lax.rem(r + 1, rows_n), lax.rem(r + rows_n - 1, rows_n)
    core = lax.rem(r, 2)
    sib = r + 1 - 2 * core
    blocks, cap, size, _ = hv.shape
    group = 2 * blocks
    total = rows_n * group
    heavy_slots = cap - LIGHT
    half_rows = blocks // 2

    barrier = pltpu.get_barrier_semaphore()
    for target in ({"row": left}, {"row": right}, {"col": 1 - y}):
        pl.semaphore_signal(barrier, inc=1, device_id=target, device_id_type=MESH)

    own_copy = pltpu.make_async_copy(h_ref, hv, loc.at[0])
    vector_copy = pltpu.make_async_copy(v_hbm, v_ref, loc.at[1])
    weight_copy = pltpu.make_async_copy(w_hbm, w_ref, loc.at[2])
    own_copy.start()
    vector_copy.start()
    weight_copy.start()
    pl.semaphore_wait(barrier, 3)

    def remote(src, dst, index, target):
        return pltpu.make_async_remote_copy(
            src_ref=src, dst_ref=dst, send_sem=send.at[index], recv_sem=recv.at[index],
            device_id=target, device_id_type=MESH,
        )

    peer = {"col": 1 - y}
    sibling = {"row": sib}
    cols_copy = remote(colsh_ref, colsp, 0, peer)
    counts_copy = remote(countsh_ref, countsp, 6 + 2 * ITERS, peer)
    light_copy = remote(h_ref.at[:, pl.ds(0, LIGHT)], hr, 1, peer)
    merge_copy = remote(
        h_ref.at[pl.ds(half_rows * (1 - core), half_rows), pl.ds(LIGHT, heavy_slots)], es, 2, sibling
    )
    mine = pl.ds(half_rows * core, half_rows)
    cross_copy = remote(em, er.at[mine], 3, peer)
    share_copy = remote(er.at[mine], er.at[mine], 4, sibling)
    check_copy = remote(cs_s, cs_r, 5, peer)

    def halo_copies(source, step):
        own_rows = group * size
        to_right = remote(
            source.at[pl.ds(own_rows - REACH * size, REACH * size)],
            halo.at[step, pl.ds(0, REACH * size)], 6 + 2 * step, {"row": right},
        )
        to_left = remote(
            source.at[pl.ds(0, RIGHT_REACH * size)],
            halo.at[step, pl.ds(REACH * size, RIGHT_REACH * size)], 7 + 2 * step, {"row": left},
        )
        return to_right, to_left

    cols_copy.start()
    counts_copy.start()
    merge_copy.start()
    light_copy.start()
    first = halo_copies(v_hbm, 0)
    first[0].start()
    first[1].start()

    def put_window(source, src_at, dst_at, count):
        def one(i, _):
            at = pl.multiple_of(src_at + i * size, size)
            high, low = split2(source[pl.ds(at, size), :])
            win[dst_at + i, :, pl.ds(0, size)] = high
            win[dst_at + i, :, pl.ds(size, size)] = low
            return 0

        lax.fori_loop(0, count, one, 0, unroll=True)

    def put_halo(step):
        put_window(halo.at[step], 0, 0, REACH)
        put_window(halo.at[step], REACH * size, REACH + group, RIGHT_REACH)

    def scalar(i, j):
        return cols_ref[i, j], colsp[i, j]

    own_is_heavy = beyond(counts_ref[0, 0], LIGHT)
    own_heavy = own_is_heavy.astype(jnp.float32)

    own_copy.wait()
    merge_copy.wait_recv()

    def merge(i, _):
        a = hv[half_rows * core + i, pl.ds(LIGHT, heavy_slots)]
        em[i] = a * own_heavy + es[i] * (1.0 - own_heavy)
        return 0

    lax.fori_loop(0, half_rows, merge, 0, unroll=True)
    cross_copy.start()

    def put_light(source, table, half):
        def one(i, _):
            count = table[0, i]
            for j in range(LIGHT):
                live = beyond(count, j).astype(jnp.float32)
                high, low = split2(source[i, j] * live)
                a_ref[half * blocks + i, pl.ds(0, size), pl.ds(j * size, size)] = high
                a_ref[half * blocks + i, pl.ds(size, size), pl.ds(j * size, size)] = low
            return 0

        lax.fori_loop(0, blocks, one, 0, unroll=True)

    vector_copy.wait()
    put_light(hv, counts_ref, y)
    put_window(v_ref, 0, REACH, group)

    cols_copy.wait_recv()
    counts_copy.wait_recv()
    peer_heavy = beyond(countsp[0, 0], LIGHT).astype(jnp.float32)

    first[0].wait_recv()
    first[1].wait_recv()
    put_halo(0)

    light_copy.wait_recv()
    put_light(hr, countsp, 1 - y)

    cross_copy.wait_recv()
    share_copy.start()
    share_copy.wait_recv()

    def put_heavy(i, _):
        own_count, peer_count = counts_ref[0, i], countsp[0, i]
        for j in range(heavy_slots):
            own_live = beyond(own_count, LIGHT + j).astype(jnp.float32)
            peer_live = beyond(peer_count, LIGHT + j).astype(jnp.float32) * (1.0 - own_heavy)
            high, low = split2(hv[i, LIGHT + j] * own_live + er[i, j] * peer_live)
            ea_ref[i, pl.ds(0, size), pl.ds(j * size, size)] = high
            ea_ref[i, pl.ds(size, size), pl.ds(j * size, size)] = low
        return 0

    lax.fori_loop(0, blocks, put_heavy, 0, unroll=True)

    base = r * group - REACH + total

    def tile(col):
        return win[jnp.minimum(lax.rem(col - base + 2 * total, total), win.shape[0] - 1)]

    def product(matrix, cols):
        tiles = jnp.concatenate([tile(col) for col in cols], 0)
        full = jnp.dot(matrix, tiles, preferred_element_type=jnp.float32)
        big = full[:size, :size]
        small = full[:size, size:] + full[size:, :size] + full[size:, size:]
        return big + small

    def heavy_products():
        def one(i, _):
            cols = []
            for j in range(heavy_slots):
                own_col, peer_col = scalar(i, LIGHT + j)
                cols.append(peer_col + own_is_heavy * (own_col - peer_col))
            p_ref[i] = product(ea_ref[i], cols)
            return 0

        lax.fori_loop(0, blocks, one, 0, unroll=True)

    def rows(half, source, older, target):
        mine = y * half + (1 - y) * (1 - half)
        share = mine.astype(jnp.float32)
        flag = own_heavy * share + peer_heavy * (1.0 - share)

        def one(i, _):
            cols = []
            for j in range(LIGHT):
                own_col, peer_col = scalar(i, j)
                cols.append(peer_col + mine * (own_col - peer_col))
            image = product(a_ref[half * blocks + i], cols) + p_ref[i] * flag
            at = pl.ds(pl.multiple_of((half * blocks + i) * size, size), size)
            value = (image - CENTRE * source[at, :]) * (1.0 / HALF_WIDTH)
            if older is not None:
                value = 2.0 * value - older[at, :]
            target[at, :] = value
            return 0

        lax.fori_loop(0, blocks, one, 0, unroll=True)

    chain = ((v_ref, None, y1), (y1, v_ref, y2), (y2, y1, out_ref))
    started = [*first]
    for step in range(ITERS):
        source, older, target = chain[step]
        if step:
            put_window(source, 0, REACH, group)
            started[2 * step].wait_recv()
            started[2 * step + 1].wait_recv()
            put_halo(step)
        heavy_products()
        if step < ITERS - 1:
            following = halo_copies(target, step + 1)
            started += following
            rows(1, source, older, target)
            following[0].start()
            rows(0, source, older, target)
            following[1].start()
        else:
            rows(1, source, older, target)
            rows(0, source, older, target)

    weight_copy.wait()
    weights = jnp.where(y == 0, w_ref[:, :size], w_ref[:, size:])
    w_high, w_rest = split2(weights)
    w_low = (weights - w_high.astype(jnp.float32) - w_rest.astype(jnp.float32)).astype(jnp.bfloat16)
    w_parts = jnp.concatenate([w_high, w_rest, w_low, jnp.zeros((13, size), jnp.bfloat16)], 0)

    def partial(half):
        at = pl.ds(pl.multiple_of(half * blocks * size, size), blocks * size)
        total_dot = 0.0
        for part in split2(out_ref[at, :]):
            total_dot += lax.dot_general(
                w_parts, part, (((1,), (1,)), ((), ())), preferred_element_type=jnp.float32
            )
        return jnp.sum(total_dot, 0, keepdims=True)

    cs_s[...] = partial(1 - y)
    check_copy.start()
    own_part = partial(y)
    check_copy.wait_recv()
    chk_ref[...] = own_part + cs_r[...]

    for copy in (cols_copy, counts_copy, light_copy, merge_copy, cross_copy, share_copy, check_copy, *started):
        copy.wait_send()


def columns_split(start_vectors, ham_blocks, block_cols, block_counts, check_weights):
    blocks, cap, size, _ = ham_blocks.shape
    rows_n = lax.axis_size("row")
    group = 2 * blocks
    height, width = start_vectors.shape
    counts = block_counts.reshape(1, blocks)
    window = REACH + group + RIGHT_REACH
    f32, bf16 = jnp.float32, jnp.bfloat16
    heavy = cap - LIGHT
    vmem = pl.BlockSpec(memory_space=pltpu.VMEM)
    smem = pl.BlockSpec(memory_space=pltpu.SMEM)
    anywhere = pl.BlockSpec(memory_space=pl.ANY)
    filtered, check = pl.pallas_call(
        functools.partial(filter_kernel, rows_n),
        out_shape=(
            jax.ShapeDtypeStruct((height, width), f32),
            jax.ShapeDtypeStruct((1, blocks * size), f32),
        ),
        in_specs=[anywhere, anywhere, smem, smem, anywhere, anywhere, anywhere],
        out_specs=(vmem, vmem),
        scratch_shapes=[
            pltpu.VMEM((height, width), f32),
            pltpu.VMEM((1, 2 * width), f32),
            pltpu.VMEM((blocks, cap, size, size), f32),
            pltpu.VMEM((blocks, LIGHT, size, size), f32),
            pltpu.VMEM((blocks // 2, heavy, size, size), f32),
            pltpu.VMEM((blocks // 2, heavy, size, size), f32),
            pltpu.VMEM((blocks, heavy, size, size), f32),
            pltpu.SMEM((blocks, cap), jnp.int32),
            pltpu.SMEM((1, blocks), jnp.int32),
            pltpu.VMEM((group, 2 * size, LIGHT * size), bf16),
            pltpu.VMEM((blocks, 2 * size, heavy * size), bf16),
            pltpu.VMEM((window, size, 2 * width), bf16),
            pltpu.VMEM((blocks, size, width), f32),
            pltpu.VMEM((height, width), f32),
            pltpu.VMEM((height, width), f32),
            pltpu.VMEM((ITERS, (REACH + RIGHT_REACH) * size, width), f32),
            pltpu.VMEM((1, blocks * size), f32),
            pltpu.VMEM((1, blocks * size), f32),
            pltpu.SemaphoreType.DMA((7 + 2 * ITERS,)),
            pltpu.SemaphoreType.DMA((7 + 2 * ITERS,)),
            pltpu.SemaphoreType.DMA((3,)),
        ],
        compiler_params=pltpu.CompilerParams(
            collective_id=0, has_side_effects=True, vmem_limit_bytes=60 * 1024 * 1024
        ),
    )(start_vectors, ham_blocks, block_cols, counts, block_cols, counts, check_weights.reshape(1, -1))
    return (filtered, check.reshape(-1))


def solution(mesh):
    placed = (
        P("row", "col"),
        P(("row", "col"), None, None, None),
        P(("row", "col"), None),
        P(("row", "col")),
        P(),
    )
    devices = mesh.shape["row"] * mesh.shape["col"]
    one_heavy = devices < 64 and mesh.shape["col"] == 2 and mesh.shape["row"] >= 4 and mesh.shape["row"] % 2 == 0
    return jax.shard_map(
        columns_split if one_heavy else rows_split,
        mesh=mesh,
        in_specs=placed,
        out_specs=(P("row", "col"), P(("row", "col"))),
        check_vma=False,
    )
```

```python
import functools

import jax
import jax.numpy as jnp
from jax import lax
from jax.experimental import pallas as pl
from jax.experimental.pallas import tpu as pltpu
from jax.sharding import PartitionSpec as P

REACH = 4
RIGHT_REACH = 3
LIGHT = 3
ITERS = 3


CENTRE = 0.25
HALF_WIDTH = 1.5
HIGHEST_PRECISION = lax.Precision.HIGHEST
MESH = pl.DeviceIdType.MESH


def shifted_2(value, axis, steps):
    count = lax.axis_size(axis)
    pairs = [(source, (source + steps) % count) for source in range(count)]
    return lax.ppermute(value, axis, pairs)


def accumulate(ham_blocks, block_cols, finishes, window, window_check, base_block, total_blocks):
    block_size = ham_blocks.shape[2]
    vector_width = window.shape[1]
    results = []
    result_checks = []
    for row_index in range(ham_blocks.shape[0]):
        matrices = ham_blocks[row_index]
        columns = block_cols[row_index]

        def add_block(slot_index, carried, matrices=matrices, columns=columns):
            summed, summed_check = carried
            offset = jnp.mod(columns[slot_index] - base_block, total_blocks) * block_size
            segment = lax.dynamic_slice_in_dim(window, offset, block_size, 0)
            segment_check = lax.dynamic_slice_in_dim(window_check, offset, block_size, 0)
            matrix = lax.dynamic_index_in_dim(matrices, slot_index, 0, keepdims=False)
            summed = summed + jnp.dot(
                matrix, segment, precision=HIGHEST_PRECISION, preferred_element_type=jnp.float32
            )
            summed_check = summed_check + jnp.dot(
                matrix,
                segment_check,
                precision=HIGHEST_PRECISION,
                preferred_element_type=jnp.float32,
            )
            return (summed, summed_check)

        initial = (
            jnp.zeros((block_size, vector_width), jnp.float32),
            jnp.zeros((block_size,), jnp.float32),
        )
        summed, summed_check = lax.fori_loop(0, finishes[row_index], add_block, initial)
        results.append(summed)
        result_checks.append(summed_check)
    return (jnp.concatenate(results, 0), jnp.concatenate(result_checks, 0))


def near_window(vectors, checks, reach_devices):
    pieces = []
    piece_checks = []
    for distance in range(-reach_devices, reach_devices + 1):
        if distance == 0:
            pieces.append(vectors)
            piece_checks.append(checks)
        else:
            shifted, shifted_check = shifted_2((vectors, checks), ("row", "col"), -distance)
            pieces.append(shifted)
            piece_checks.append(shifted_check)
    return (jnp.concatenate(pieces, 0), jnp.concatenate(piece_checks, 0))


def rows_split(start_vectors, ham_blocks, block_cols, block_counts, check_weights):
    row_vectors = lax.all_to_all(start_vectors, "col", split_axis=0, concat_axis=1, tiled=True)
    checks = jnp.dot(
        row_vectors, check_weights, precision=HIGHEST_PRECISION, preferred_element_type=jnp.float32
    )
    blocks_here = ham_blocks.shape[0]
    total_blocks = lax.axis_size(("row", "col")) * blocks_here
    position = lax.axis_index(("row", "col"))
    neighbours = (REACH + blocks_here - 1) // blocks_here
    base_block = (position - neighbours) * blocks_here

    def apply_operator(vectors, vector_checks):
        window, window_check = near_window(vectors, vector_checks, neighbours)
        return accumulate(
            ham_blocks, block_cols, block_counts, window, window_check, base_block, total_blocks
        )

    previous, previous_check = (row_vectors, checks)
    image_rows, image_check = apply_operator(row_vectors, checks)
    current = (image_rows - CENTRE * row_vectors) / HALF_WIDTH
    current_check = (image_check - CENTRE * checks) / HALF_WIDTH
    for step_index in range(ITERS - 1):
        image_rows, image_check = apply_operator(current, current_check)
        following = 2.0 * (image_rows - CENTRE * current) / HALF_WIDTH - previous
        following_check = 2.0 * (image_check - CENTRE * current_check) / HALF_WIDTH - previous_check
        previous, previous_check = (current, current_check)
        current, current_check = (following, following_check)
    filtered = lax.all_to_all(current, "col", split_axis=1, concat_axis=0, tiled=True)
    return (filtered, current_check)


def split2(x):
    high = x.astype(jnp.bfloat16)
    low = (x - high.astype(jnp.float32)).astype(jnp.bfloat16)
    return high, low


def beyond(count, slot):
    return jnp.minimum(jnp.maximum(count - slot, 0), 1)


def filter_kernel(
    rows_n, v_hbm, h_ref, cols_ref, counts_ref, colsh_ref, countsh_ref, w_hbm, out_ref, chk_ref,
    v_ref, w_ref, hv, hr, st, es, em, ex, ec, er, colsp, countsp, a_ref, ea_ref, win, p_ref, y1, y2,
    halo, cs_s, cs_r, send, recv, loc,
):
    r = lax.axis_index("row")
    y = lax.axis_index("col")
    right, left = lax.rem(r + 1, rows_n), lax.rem(r + rows_n - 1, rows_n)
    core = lax.rem(r, 2)
    pair = lax.rem(r // 2, 2)
    blocks, cap, size, _ = hv.shape
    group = 2 * blocks
    total = rows_n * group
    heavy_slots = cap - LIGHT
    half_rows = blocks // 2
    peer = {"col": 1 - y}
    sibling = {"row": r + 1 - 2 * core}
    across = {"row": r + 2 - 4 * pair}

    barrier = pltpu.get_barrier_semaphore()
    for target in ({"row": left}, {"row": right}, across, peer):
        pl.semaphore_signal(barrier, inc=1, device_id=target, device_id_type=MESH)

    own_copy = pltpu.make_async_copy(h_ref, hv, loc.at[0])
    vector_copy = pltpu.make_async_copy(v_hbm, v_ref, loc.at[1])
    weight_copy = pltpu.make_async_copy(w_hbm, w_ref, loc.at[2])
    own_copy.start()
    vector_copy.start()
    weight_copy.start()
    pl.semaphore_wait(barrier, 4)

    def remote(src, dst, index, target):
        return pltpu.make_async_remote_copy(
            src_ref=src, dst_ref=dst, send_sem=send.at[index], recv_sem=recv.at[index],
            device_id=target, device_id_type=MESH,
        )

    mine_row = half_rows * core + pair
    other_row = half_rows * core + 1 - pair
    cols_copy = remote(colsh_ref, colsp, 0, peer)
    counts_copy = remote(countsh_ref, countsp, 1, peer)

    def light_part(part):
        at = pl.ds(half_rows * part, half_rows)
        return remote(h_ref.at[at, pl.ds(0, LIGHT)], hr.at[at], 2 + part, peer)

    light_copies = (light_part(0), light_part(1))
    chip_copy = remote(st, es, 4, sibling)
    pair_copy = remote(em.at[1 - pair], ex, 5, across)
    cross_copy = remote(ec, er.at[mine_row], 6, peer)
    pair_share = remote(er.at[mine_row], er.at[mine_row], 7, across)
    chip_share = remote(er.at[mine_row], er.at[mine_row], 8, sibling)
    chip_share_2 = remote(er.at[other_row], er.at[other_row], 9, sibling)
    check_copy = remote(cs_s, cs_r, 10, peer)

    def halo_copies(source, step):
        own_rows = group * size
        to_right = remote(
            source.at[pl.ds(own_rows - REACH * size, REACH * size)],
            halo.at[step, pl.ds(0, REACH * size)], 11 + 2 * step, {"row": right},
        )
        to_left = remote(
            source.at[pl.ds(0, RIGHT_REACH * size)],
            halo.at[step, pl.ds(REACH * size, RIGHT_REACH * size)], 12 + 2 * step, {"row": left},
        )
        return to_right, to_left

    cols_copy.start()
    counts_copy.start()
    light_copies[0].start()

    def loop(count, body):
        def one(i, carry):
            body(i)
            return carry

        lax.fori_loop(0, count, one, 0, unroll=True)

    def put_window(source, src_at, dst_at, count):
        def one(i):
            at = pl.multiple_of(src_at + i * size, size)
            high, low = split2(source[pl.ds(at, size), :])
            win[dst_at + i, :, pl.ds(0, size)] = high
            win[dst_at + i, :, pl.ds(size, size)] = low

        loop(count, one)

    def put_halo(step):
        put_window(halo.at[step], 0, 0, REACH)
        put_window(halo.at[step], REACH * size, REACH + group, RIGHT_REACH)

    own_is_heavy = beyond(counts_ref[0, 0], LIGHT)
    own_heavy = own_is_heavy.astype(jnp.float32)

    own_copy.wait()

    def stage(i):
        st[i] = hv[half_rows * (1 - core) + i, pl.ds(LIGHT, heavy_slots)] * own_heavy

    loop(half_rows, stage)
    chip_copy.start()

    def put_light(source, table, half, first_row, count):
        def one(i):
            i = first_row + i
            live_count = table[0, i]
            for j in range(LIGHT):
                live = beyond(live_count, j).astype(jnp.float32)
                high, low = split2(source[i, j] * live)
                a_ref[half * blocks + i, pl.ds(0, size), pl.ds(j * size, size)] = high
                a_ref[half * blocks + i, pl.ds(size, size), pl.ds(j * size, size)] = low

        loop(count, one)

    def put_heavy(with_peer):
        def one(i):
            for j in range(heavy_slots):
                live = beyond(counts_ref[0, i], LIGHT + j).astype(jnp.float32)
                value = hv[i, LIGHT + j] * live
                if with_peer:
                    live = beyond(countsp[0, i], LIGHT + j).astype(jnp.float32) * (1.0 - own_heavy)
                    value = value + er[i, j] * live
                high, low = split2(value)
                ea_ref[i, pl.ds(0, size), pl.ds(j * size, size)] = high
                ea_ref[i, pl.ds(size, size), pl.ds(j * size, size)] = low

        loop(blocks, one)

    put_light(hv, counts_ref, y, 0, blocks)
    chip_copy.wait_recv()

    def merge(i):
        em[i] = hv[half_rows * core + i, pl.ds(LIGHT, heavy_slots)] * own_heavy + es[i]

    loop(half_rows, merge)
    pair_copy.start()

    put_heavy(False)
    vector_copy.wait()
    put_window(v_ref, 0, REACH, group)
    cols_copy.wait_recv()
    counts_copy.wait_recv()
    peer_heavy = beyond(countsp[0, 0], LIGHT).astype(jnp.float32)

    pair_copy.wait_recv()
    ec[...] = em[pair] + ex[...]
    cross_copy.start()
    first = halo_copies(v_hbm, 0)
    first[0].start()
    first[1].start()
    cross_copy.wait_send()
    light_copies[1].start()

    base = r * group - REACH + total

    def tile(col):
        return win[jnp.minimum(lax.rem(col - base + 2 * total, total), win.shape[0] - 1)]

    def product(matrix, cols):
        tiles = jnp.concatenate([tile(col) for col in cols], 0)
        full = jnp.dot(matrix, tiles, preferred_element_type=jnp.float32)
        big = full[:size, :size]
        small = full[:size, size:] + full[size:, :size] + full[size:, size:]
        return big + small

    def heavy_products():
        def one(i):
            cols = []
            for j in range(LIGHT, cap):
                own_col, peer_col = cols_ref[i, j], colsp[i, j]
                cols.append(peer_col + own_is_heavy * (own_col - peer_col))
            p_ref[i] = product(ea_ref[i], cols)

        loop(blocks, one)

    def place(half, i):
        return pl.ds(pl.multiple_of((half * blocks + i) * size, size), size)

    def rows(half, source, older, target, first_row=0, count=blocks, heavy=True):
        mine = y * half + (1 - y) * (1 - half)
        share = mine.astype(jnp.float32)
        flag = own_heavy * share + peer_heavy * (1.0 - share)

        def one(i):
            i = first_row + i
            cols = []
            for j in range(LIGHT):
                own_col, peer_col = cols_ref[i, j], colsp[i, j]
                cols.append(peer_col + mine * (own_col - peer_col))
            image = product(a_ref[half * blocks + i], cols)
            if heavy:
                image = image + p_ref[i] * flag
            at = place(half, i)
            value = (image - CENTRE * source[at, :]) * (1.0 / HALF_WIDTH)
            if older is not None:
                value = 2.0 * value - older[at, :]
            target[at, :] = value

        loop(count, one)

    first[0].wait_recv()
    first[1].wait_recv()
    put_halo(0)
    heavy_products()
    rows(y, v_ref, None, y1)
    second = halo_copies(y1, 1)

    @pl.when(y == 1)
    def _():
        second[0].start()

    @pl.when(y == 0)
    def _():
        second[1].start()

    cross_copy.wait_recv()
    pair_share.start()
    chip_share.start()
    light_copies[0].wait_recv()
    put_light(hr, countsp, 1 - y, 0, half_rows)
    rows(1 - y, v_ref, None, y1, 0, half_rows, False)
    pair_share.wait_recv()
    chip_share_2.start()
    light_copies[1].wait_recv()
    put_light(hr, countsp, 1 - y, half_rows, blocks - half_rows)
    rows(1 - y, v_ref, None, y1, half_rows, blocks - half_rows, False)
    chip_share.wait_recv()
    chip_share_2.wait_recv()
    put_heavy(True)
    heavy_products()

    def add_heavy(i):
        at = place(1 - y, i)
        y1[at, :] = y1[at, :] + p_ref[i] * (peer_heavy * (1.0 / HALF_WIDTH))

    loop(blocks, add_heavy)

    @pl.when(y == 0)
    def _():
        second[0].start()

    @pl.when(y == 1)
    def _():
        second[1].start()

    chain = ((v_ref, None, y1), (y1, v_ref, y2), (y2, y1, out_ref))
    started = [*first, *second]
    for step in range(1, ITERS):
        source, older, target = chain[step]
        put_window(source, 0, REACH, group)
        started[2 * step].wait_recv()
        started[2 * step + 1].wait_recv()
        put_halo(step)
        heavy_products()
        if step < ITERS - 1:
            following = halo_copies(target, step + 1)
            started += following
            rows(1, source, older, target)
            following[0].start()
            rows(0, source, older, target)
            following[1].start()
        else:
            rows(1, source, older, target)
            rows(0, source, older, target)

    weight_copy.wait()
    weights = jnp.where(y == 0, w_ref[:, :size], w_ref[:, size:])
    w_high, w_rest = split2(weights)
    w_low = (weights - w_high.astype(jnp.float32) - w_rest.astype(jnp.float32)).astype(jnp.bfloat16)
    w_parts = jnp.concatenate([w_high, w_rest, w_low, jnp.zeros((13, size), jnp.bfloat16)], 0)

    def partial(half):
        at = pl.ds(pl.multiple_of(half * blocks * size, size), blocks * size)
        total_dot = 0.0
        for part in split2(out_ref[at, :]):
            total_dot += lax.dot_general(
                w_parts, part, (((1,), (1,)), ((), ())), preferred_element_type=jnp.float32
            )
        return jnp.sum(total_dot, 0, keepdims=True)

    cs_s[...] = partial(1 - y)
    check_copy.start()
    own_part = partial(y)
    check_copy.wait_recv()
    chk_ref[...] = own_part + cs_r[...]

    for copy in (
        cols_copy, counts_copy, *light_copies, chip_copy, pair_copy, pair_share, chip_share,
        chip_share_2, check_copy, *started,
    ):
        copy.wait_send()


def columns_split(start_vectors, ham_blocks, block_cols, block_counts, check_weights):
    blocks, cap, size, _ = ham_blocks.shape
    rows_n = lax.axis_size("row")
    group = 2 * blocks
    height, width = start_vectors.shape
    counts = block_counts.reshape(1, blocks)
    window = REACH + group + RIGHT_REACH
    f32, bf16 = jnp.float32, jnp.bfloat16
    heavy = cap - LIGHT
    vmem = pl.BlockSpec(memory_space=pltpu.VMEM)
    smem = pl.BlockSpec(memory_space=pltpu.SMEM)
    anywhere = pl.BlockSpec(memory_space=pl.ANY)
    filtered, check = pl.pallas_call(
        functools.partial(filter_kernel, rows_n),
        out_shape=(
            jax.ShapeDtypeStruct((height, width), f32),
            jax.ShapeDtypeStruct((1, blocks * size), f32),
        ),
        in_specs=[anywhere, anywhere, smem, smem, anywhere, anywhere, anywhere],
        out_specs=(vmem, vmem),
        scratch_shapes=[
            pltpu.VMEM((height, width), f32),
            pltpu.VMEM((1, 2 * width), f32),
            pltpu.VMEM((blocks, cap, size, size), f32),
            pltpu.VMEM((blocks, LIGHT, size, size), f32),
            pltpu.VMEM((blocks // 2, heavy, size, size), f32),
            pltpu.VMEM((blocks // 2, heavy, size, size), f32),
            pltpu.VMEM((blocks // 2, heavy, size, size), f32),
            pltpu.VMEM((heavy, size, size), f32),
            pltpu.VMEM((heavy, size, size), f32),
            pltpu.VMEM((blocks, heavy, size, size), f32),
            pltpu.SMEM((blocks, cap), jnp.int32),
            pltpu.SMEM((1, blocks), jnp.int32),
            pltpu.VMEM((group, 2 * size, LIGHT * size), bf16),
            pltpu.VMEM((blocks, 2 * size, heavy * size), bf16),
            pltpu.VMEM((window, size, 2 * width), bf16),
            pltpu.VMEM((blocks, size, width), f32),
            pltpu.VMEM((height, width), f32),
            pltpu.VMEM((height, width), f32),
            pltpu.VMEM((ITERS, (REACH + RIGHT_REACH) * size, width), f32),
            pltpu.VMEM((1, blocks * size), f32),
            pltpu.VMEM((1, blocks * size), f32),
            pltpu.SemaphoreType.DMA((11 + 2 * ITERS,)),
            pltpu.SemaphoreType.DMA((11 + 2 * ITERS,)),
            pltpu.SemaphoreType.DMA((3,)),
        ],
        compiler_params=pltpu.CompilerParams(
            collective_id=0, has_side_effects=True, vmem_limit_bytes=60 * 1024 * 1024
        ),
    )(start_vectors, ham_blocks, block_cols, counts, block_cols, counts, check_weights.reshape(1, -1))
    return (filtered, check.reshape(-1))


def solution(mesh):
    placed = (
        P("row", "col"),
        P(("row", "col"), None, None, None),
        P(("row", "col"), None),
        P(("row", "col")),
        P(),
    )
    devices = mesh.shape["row"] * mesh.shape["col"]
    one_heavy = devices < 64 and mesh.shape["col"] == 2 and mesh.shape["row"] >= 8 and mesh.shape["row"] % 4 == 0
    return jax.shard_map(
        columns_split if one_heavy else rows_split,
        mesh=mesh,
        in_specs=placed,
        out_specs=(P("row", "col"), P(("row", "col"))),
        check_vma=False,
    )
```

```python
import functools

import jax
import jax.numpy as jnp
from jax import lax
from jax.experimental import pallas as pl
from jax.experimental.pallas import tpu as pltpu
from jax.sharding import PartitionSpec as P

REACH = 4
RIGHT_REACH = 3
LIGHT = 3
ITERS = 3


CENTRE = 0.25
HALF_WIDTH = 1.5
HIGHEST_PRECISION = lax.Precision.HIGHEST
MESH = pl.DeviceIdType.MESH


def shifted_2(value, axis, steps):
    count = lax.axis_size(axis)
    pairs = [(source, (source + steps) % count) for source in range(count)]
    return lax.ppermute(value, axis, pairs)


def accumulate(ham_blocks, block_cols, finishes, window, window_check, base_block, total_blocks):
    block_size = ham_blocks.shape[2]
    vector_width = window.shape[1]
    results = []
    result_checks = []
    for row_index in range(ham_blocks.shape[0]):
        matrices = ham_blocks[row_index]
        columns = block_cols[row_index]

        def add_block(slot_index, carried, matrices=matrices, columns=columns):
            summed, summed_check = carried
            offset = jnp.mod(columns[slot_index] - base_block, total_blocks) * block_size
            segment = lax.dynamic_slice_in_dim(window, offset, block_size, 0)
            segment_check = lax.dynamic_slice_in_dim(window_check, offset, block_size, 0)
            matrix = lax.dynamic_index_in_dim(matrices, slot_index, 0, keepdims=False)
            summed = summed + jnp.dot(
                matrix, segment, precision=HIGHEST_PRECISION, preferred_element_type=jnp.float32
            )
            summed_check = summed_check + jnp.dot(
                matrix,
                segment_check,
                precision=HIGHEST_PRECISION,
                preferred_element_type=jnp.float32,
            )
            return (summed, summed_check)

        initial = (
            jnp.zeros((block_size, vector_width), jnp.float32),
            jnp.zeros((block_size,), jnp.float32),
        )
        summed, summed_check = lax.fori_loop(0, finishes[row_index], add_block, initial)
        results.append(summed)
        result_checks.append(summed_check)
    return (jnp.concatenate(results, 0), jnp.concatenate(result_checks, 0))


def near_window(vectors, checks, reach_devices):
    pieces = []
    piece_checks = []
    for distance in range(-reach_devices, reach_devices + 1):
        if distance == 0:
            pieces.append(vectors)
            piece_checks.append(checks)
        else:
            shifted, shifted_check = shifted_2((vectors, checks), ("row", "col"), -distance)
            pieces.append(shifted)
            piece_checks.append(shifted_check)
    return (jnp.concatenate(pieces, 0), jnp.concatenate(piece_checks, 0))


def rows_split(start_vectors, ham_blocks, block_cols, block_counts, check_weights):
    row_vectors = lax.all_to_all(start_vectors, "col", split_axis=0, concat_axis=1, tiled=True)
    checks = jnp.dot(
        row_vectors, check_weights, precision=HIGHEST_PRECISION, preferred_element_type=jnp.float32
    )
    blocks_here = ham_blocks.shape[0]
    total_blocks = lax.axis_size(("row", "col")) * blocks_here
    position = lax.axis_index(("row", "col"))
    neighbours = (REACH + blocks_here - 1) // blocks_here
    base_block = (position - neighbours) * blocks_here

    def apply_operator(vectors, vector_checks):
        window, window_check = near_window(vectors, vector_checks, neighbours)
        return accumulate(
            ham_blocks, block_cols, block_counts, window, window_check, base_block, total_blocks
        )

    previous, previous_check = (row_vectors, checks)
    image_rows, image_check = apply_operator(row_vectors, checks)
    current = (image_rows - CENTRE * row_vectors) / HALF_WIDTH
    current_check = (image_check - CENTRE * checks) / HALF_WIDTH
    for step_index in range(ITERS - 1):
        image_rows, image_check = apply_operator(current, current_check)
        following = 2.0 * (image_rows - CENTRE * current) / HALF_WIDTH - previous
        following_check = 2.0 * (image_check - CENTRE * current_check) / HALF_WIDTH - previous_check
        previous, previous_check = (current, current_check)
        current, current_check = (following, following_check)
    filtered = lax.all_to_all(current, "col", split_axis=1, concat_axis=0, tiled=True)
    return (filtered, current_check)


def split2(x):
    high = x.astype(jnp.bfloat16)
    low = (x - high.astype(jnp.float32)).astype(jnp.bfloat16)
    return high, low


def beyond(count, slot):
    return jnp.minimum(jnp.maximum(count - slot, 0), 1)


def filter_kernel(
    rows_n, v_hbm, h_ref, cols_ref, counts_ref, colsh_ref, countsh_ref, w_hbm, out_ref, chk_ref,
    v_ref, w_ref, hv, hr, st, es, em, ex, ec, er, colsp, countsp, a_ref, ea_ref, win, p_ref, y1, y2,
    halo, cs_s, cs_r, send, recv, loc,
):
    r = lax.axis_index("row")
    y = lax.axis_index("col")
    right, left = lax.rem(r + 1, rows_n), lax.rem(r + rows_n - 1, rows_n)
    core = lax.rem(r, 2)
    pair = lax.rem(r // 2, 2)
    blocks, cap, size, _ = hv.shape
    group = 2 * blocks
    total = rows_n * group
    heavy_slots = cap - LIGHT
    half_rows = blocks // 2
    peer = {"col": 1 - y}
    sibling = {"row": r + 1 - 2 * core}
    across = {"row": r + 2 - 4 * pair}

    barrier = pltpu.get_barrier_semaphore()
    for target in ({"row": left}, {"row": right}, across, peer):
        pl.semaphore_signal(barrier, inc=1, device_id=target, device_id_type=MESH)

    own_copy = pltpu.make_async_copy(h_ref, hv, loc.at[0])
    vector_copy = pltpu.make_async_copy(v_hbm, v_ref, loc.at[1])
    weight_copy = pltpu.make_async_copy(w_hbm, w_ref, loc.at[2])
    own_copy.start()
    vector_copy.start()
    weight_copy.start()
    pl.semaphore_wait(barrier, 4)

    def remote(src, dst, index, target):
        return pltpu.make_async_remote_copy(
            src_ref=src, dst_ref=dst, send_sem=send.at[index], recv_sem=recv.at[index],
            device_id=target, device_id_type=MESH,
        )

    mine_row = half_rows * core + pair
    other_row = half_rows * core + 1 - pair
    cols_copy = remote(colsh_ref, colsp, 0, peer)
    counts_copy = remote(countsh_ref, countsp, 1, peer)

    def light_part(part):
        at = pl.ds(half_rows * part, half_rows)
        return remote(h_ref.at[at, pl.ds(0, LIGHT)], hr.at[at], 2 + part, peer)

    light_copies = (light_part(0), light_part(1))
    chip_copy = remote(st, es, 4, sibling)
    pair_copy = remote(em.at[1 - pair], ex, 5, across)
    cross_copy = remote(ec, er.at[mine_row], 6, peer)
    pair_share = remote(er.at[mine_row], er.at[mine_row], 7, across)
    chip_share = remote(er.at[mine_row], er.at[mine_row], 8, sibling)
    chip_share_2 = remote(er.at[other_row], er.at[other_row], 9, sibling)
    check_copy = remote(cs_s, cs_r, 10, peer)

    def halo_copies(source, step):
        own_rows = group * size
        to_right = remote(
            source.at[pl.ds(own_rows - REACH * size, REACH * size)],
            halo.at[step, pl.ds(0, REACH * size)], 11 + 2 * step, {"row": right},
        )
        to_left = remote(
            source.at[pl.ds(0, RIGHT_REACH * size)],
            halo.at[step, pl.ds(REACH * size, RIGHT_REACH * size)], 12 + 2 * step, {"row": left},
        )
        return to_right, to_left

    cols_copy.start()
    counts_copy.start()
    light_copies[0].start()

    def loop(count, body):
        def one(i, carry):
            body(i)
            return carry

        lax.fori_loop(0, count, one, 0, unroll=True)

    def put_window(source, src_at, dst_at, count):
        def one(i):
            at = pl.multiple_of(src_at + i * size, size)
            high, low = split2(source[pl.ds(at, size), :])
            win[dst_at + i, :, pl.ds(0, size)] = high
            win[dst_at + i, :, pl.ds(size, size)] = low

        loop(count, one)

    def put_halo(step):
        put_window(halo.at[step], 0, 0, REACH)
        put_window(halo.at[step], REACH * size, REACH + group, RIGHT_REACH)

    own_is_heavy = beyond(counts_ref[0, 0], LIGHT)
    own_heavy = own_is_heavy.astype(jnp.float32)

    own_copy.wait()

    def stage(i):
        st[i] = hv[half_rows * (1 - core) + i, pl.ds(LIGHT, heavy_slots)] * own_heavy

    loop(half_rows, stage)
    chip_copy.start()

    def put_light(source, table, half, first_row, count):
        def one(i):
            i = first_row + i
            live_count = table[0, i]
            for j in range(LIGHT):
                live = beyond(live_count, j).astype(jnp.float32)
                high, low = split2(source[i, j] * live)
                a_ref[half * blocks + i, pl.ds(0, size), pl.ds(j * size, size)] = high
                a_ref[half * blocks + i, pl.ds(size, size), pl.ds(j * size, size)] = low

        loop(count, one)

    def put_heavy(with_peer):
        def one(i):
            for j in range(heavy_slots):
                live = beyond(counts_ref[0, i], LIGHT + j).astype(jnp.float32)
                value = hv[i, LIGHT + j] * live
                if with_peer:
                    live = beyond(countsp[0, i], LIGHT + j).astype(jnp.float32) * (1.0 - own_heavy)
                    value = value + er[i, j] * live
                high, low = split2(value)
                ea_ref[i, pl.ds(0, size), pl.ds(j * size, size)] = high
                ea_ref[i, pl.ds(size, size), pl.ds(j * size, size)] = low

        loop(blocks, one)

    put_light(hv, counts_ref, y, 0, blocks)
    chip_copy.wait_recv()

    def merge(i):
        em[i] = hv[half_rows * core + i, pl.ds(LIGHT, heavy_slots)] * own_heavy + es[i]

    loop(half_rows, merge)
    pair_copy.start()

    put_heavy(False)
    vector_copy.wait()
    put_window(v_ref, 0, REACH, group)
    cols_copy.wait_recv()
    counts_copy.wait_recv()
    peer_heavy = beyond(countsp[0, 0], LIGHT).astype(jnp.float32)

    pair_copy.wait_recv()
    ec[...] = em[pair] + ex[...]
    cross_copy.start()
    first = halo_copies(v_hbm, 0)
    first[0].start()
    first[1].start()
    cross_copy.wait_send()
    light_copies[1].start()

    base = r * group - REACH + total

    def tile(col):
        return win[jnp.minimum(lax.rem(col - base + 2 * total, total), win.shape[0] - 1)]

    def product(matrix, cols):
        tiles = jnp.concatenate([tile(col) for col in cols], 0)
        full = jnp.dot(matrix, tiles, preferred_element_type=jnp.float32)
        big = full[:size, :size]
        small = full[:size, size:] + full[size:, :size] + full[size:, size:]
        return big + small

    def heavy_products():
        def one(i):
            cols = []
            for j in range(LIGHT, cap):
                own_col, peer_col = cols_ref[i, j], colsp[i, j]
                cols.append(peer_col + own_is_heavy * (own_col - peer_col))
            p_ref[i] = product(ea_ref[i], cols)

        loop(blocks, one)

    def place(half, i):
        return pl.ds(pl.multiple_of((half * blocks + i) * size, size), size)

    def rows(half, source, older, target, first_row=0, count=blocks, heavy=True):
        mine = y * half + (1 - y) * (1 - half)
        share = mine.astype(jnp.float32)
        flag = own_heavy * share + peer_heavy * (1.0 - share)

        def one(i):
            i = first_row + i
            cols = []
            for j in range(LIGHT):
                own_col, peer_col = cols_ref[i, j], colsp[i, j]
                cols.append(peer_col + mine * (own_col - peer_col))
            image = product(a_ref[half * blocks + i], cols)
            if heavy:
                image = image + p_ref[i] * flag
            at = place(half, i)
            value = (image - CENTRE * source[at, :]) * (1.0 / HALF_WIDTH)
            if older is not None:
                value = 2.0 * value - older[at, :]
            target[at, :] = value

        loop(count, one)

    first[0].wait_recv()
    first[1].wait_recv()
    put_halo(0)
    heavy_products()
    rows(y, v_ref, None, y1)
    second = halo_copies(y1, 1)

    @pl.when(y == 1)
    def _():
        second[0].start()

    @pl.when(y == 0)
    def _():
        second[1].start()

    cross_copy.wait_recv()
    pair_share.start()
    chip_share.start()
    light_copies[0].wait_recv()
    put_light(hr, countsp, 1 - y, 0, half_rows)
    rows(1 - y, v_ref, None, y1, 0, half_rows, False)
    pair_share.wait_recv()
    chip_share_2.start()
    light_copies[1].wait_recv()
    put_light(hr, countsp, 1 - y, half_rows, blocks - half_rows)
    rows(1 - y, v_ref, None, y1, half_rows, blocks - half_rows, False)
    chip_share.wait_recv()
    chip_share_2.wait_recv()
    put_heavy(True)
    heavy_products()

    def add_heavy(i):
        at = place(1 - y, i)
        y1[at, :] = y1[at, :] + p_ref[i] * (peer_heavy * (1.0 / HALF_WIDTH))

    loop(blocks, add_heavy)

    @pl.when(y == 0)
    def _():
        second[0].start()

    @pl.when(y == 1)
    def _():
        second[1].start()

    def take_halo(half, copies, step):
        @pl.when(half == 0)
        def _():
            copies[0].wait_recv()
            put_window(halo.at[step], 0, 0, REACH)

        @pl.when(half == 1)
        def _():
            copies[1].wait_recv()
            put_window(halo.at[step], REACH * size, REACH + group, RIGHT_REACH)

    def send_halo(half, copies):
        @pl.when(half == 1)
        def _():
            copies[0].start()

        @pl.when(half == 0)
        def _():
            copies[1].start()

    chain = ((v_ref, None, y1), (y1, v_ref, y2), (y2, y1, out_ref))
    started = [*first, *second]
    early, late = 1 - y, y
    for step in range(1, ITERS):
        source, older, target = chain[step]
        copies = started[2 * step:]
        following = halo_copies(target, step + 1) if step < ITERS - 1 else ()
        started += following
        put_window(source, 0, REACH, group)
        for half in (early, late):
            take_halo(half, copies, step)
            heavy_products()
            rows(half, source, older, target)
            if following:
                send_halo(half, following)
        early, late = late, early

    weight_copy.wait()
    weights = jnp.where(y == 0, w_ref[:, :size], w_ref[:, size:])
    w_high, w_rest = split2(weights)
    w_low = (weights - w_high.astype(jnp.float32) - w_rest.astype(jnp.float32)).astype(jnp.bfloat16)
    w_parts = jnp.concatenate([w_high, w_rest, w_low, jnp.zeros((13, size), jnp.bfloat16)], 0)

    def partial(half):
        at = pl.ds(pl.multiple_of(half * blocks * size, size), blocks * size)
        total_dot = 0.0
        for part in split2(out_ref[at, :]):
            total_dot += lax.dot_general(
                w_parts, part, (((1,), (1,)), ((), ())), preferred_element_type=jnp.float32
            )
        return jnp.sum(total_dot, 0, keepdims=True)

    cs_s[...] = partial(1 - y)
    check_copy.start()
    own_part = partial(y)
    check_copy.wait_recv()
    chk_ref[...] = own_part + cs_r[...]

    for copy in (
        cols_copy, counts_copy, *light_copies, chip_copy, pair_copy, pair_share, chip_share,
        chip_share_2, check_copy, *started,
    ):
        copy.wait_send()


def columns_split(start_vectors, ham_blocks, block_cols, block_counts, check_weights):
    blocks, cap, size, _ = ham_blocks.shape
    rows_n = lax.axis_size("row")
    group = 2 * blocks
    height, width = start_vectors.shape
    counts = block_counts.reshape(1, blocks)
    window = REACH + group + RIGHT_REACH
    f32, bf16 = jnp.float32, jnp.bfloat16
    heavy = cap - LIGHT
    vmem = pl.BlockSpec(memory_space=pltpu.VMEM)
    smem = pl.BlockSpec(memory_space=pltpu.SMEM)
    anywhere = pl.BlockSpec(memory_space=pl.ANY)
    filtered, check = pl.pallas_call(
        functools.partial(filter_kernel, rows_n),
        out_shape=(
            jax.ShapeDtypeStruct((height, width), f32),
            jax.ShapeDtypeStruct((1, blocks * size), f32),
        ),
        in_specs=[anywhere, anywhere, smem, smem, anywhere, anywhere, anywhere],
        out_specs=(vmem, vmem),
        scratch_shapes=[
            pltpu.VMEM((height, width), f32),
            pltpu.VMEM((1, 2 * width), f32),
            pltpu.VMEM((blocks, cap, size, size), f32),
            pltpu.VMEM((blocks, LIGHT, size, size), f32),
            pltpu.VMEM((blocks // 2, heavy, size, size), f32),
            pltpu.VMEM((blocks // 2, heavy, size, size), f32),
            pltpu.VMEM((blocks // 2, heavy, size, size), f32),
            pltpu.VMEM((heavy, size, size), f32),
            pltpu.VMEM((heavy, size, size), f32),
            pltpu.VMEM((blocks, heavy, size, size), f32),
            pltpu.SMEM((blocks, cap), jnp.int32),
            pltpu.SMEM((1, blocks), jnp.int32),
            pltpu.VMEM((group, 2 * size, LIGHT * size), bf16),
            pltpu.VMEM((blocks, 2 * size, heavy * size), bf16),
            pltpu.VMEM((window, size, 2 * width), bf16),
            pltpu.VMEM((blocks, size, width), f32),
            pltpu.VMEM((height, width), f32),
            pltpu.VMEM((height, width), f32),
            pltpu.VMEM((ITERS, (REACH + RIGHT_REACH) * size, width), f32),
            pltpu.VMEM((1, blocks * size), f32),
            pltpu.VMEM((1, blocks * size), f32),
            pltpu.SemaphoreType.DMA((11 + 2 * ITERS,)),
            pltpu.SemaphoreType.DMA((11 + 2 * ITERS,)),
            pltpu.SemaphoreType.DMA((3,)),
        ],
        compiler_params=pltpu.CompilerParams(
            collective_id=0, has_side_effects=True, vmem_limit_bytes=60 * 1024 * 1024
        ),
    )(start_vectors, ham_blocks, block_cols, counts, block_cols, counts, check_weights.reshape(1, -1))
    return (filtered, check.reshape(-1))


def solution(mesh):
    placed = (
        P("row", "col"),
        P(("row", "col"), None, None, None),
        P(("row", "col"), None),
        P(("row", "col")),
        P(),
    )
    devices = mesh.shape["row"] * mesh.shape["col"]
    one_heavy = devices < 64 and mesh.shape["col"] == 2 and mesh.shape["row"] >= 8 and mesh.shape["row"] % 4 == 0
    return jax.shard_map(
        columns_split if one_heavy else rows_split,
        mesh=mesh,
        in_specs=placed,
        out_specs=(P("row", "col"), P(("row", "col"))),
        check_vma=False,
    )
```

```python
import functools

import jax
import jax.numpy as jnp
from jax import lax
from jax.experimental import pallas as pl
from jax.experimental.pallas import tpu as pltpu
from jax.sharding import PartitionSpec as P

REACH = 4
RIGHT_REACH = 3
LIGHT = 3
ITERS = 3


CENTRE = 0.25
HALF_WIDTH = 1.5
HIGHEST_PRECISION = lax.Precision.HIGHEST
MESH = pl.DeviceIdType.MESH


def shifted_2(value, axis, steps):
    count = lax.axis_size(axis)
    pairs = [(source, (source + steps) % count) for source in range(count)]
    return lax.ppermute(value, axis, pairs)


def accumulate(ham_blocks, block_cols, finishes, window, window_check, base_block, total_blocks):
    block_size = ham_blocks.shape[2]
    vector_width = window.shape[1]
    results = []
    result_checks = []
    for row_index in range(ham_blocks.shape[0]):
        matrices = ham_blocks[row_index]
        columns = block_cols[row_index]

        def add_block(slot_index, carried, matrices=matrices, columns=columns):
            summed, summed_check = carried
            offset = jnp.mod(columns[slot_index] - base_block, total_blocks) * block_size
            segment = lax.dynamic_slice_in_dim(window, offset, block_size, 0)
            segment_check = lax.dynamic_slice_in_dim(window_check, offset, block_size, 0)
            matrix = lax.dynamic_index_in_dim(matrices, slot_index, 0, keepdims=False)
            summed = summed + jnp.dot(
                matrix, segment, precision=HIGHEST_PRECISION, preferred_element_type=jnp.float32
            )
            summed_check = summed_check + jnp.dot(
                matrix,
                segment_check,
                precision=HIGHEST_PRECISION,
                preferred_element_type=jnp.float32,
            )
            return (summed, summed_check)

        initial = (
            jnp.zeros((block_size, vector_width), jnp.float32),
            jnp.zeros((block_size,), jnp.float32),
        )
        summed, summed_check = lax.fori_loop(0, finishes[row_index], add_block, initial)
        results.append(summed)
        result_checks.append(summed_check)
    return (jnp.concatenate(results, 0), jnp.concatenate(result_checks, 0))


def near_window(vectors, checks, reach_devices):
    pieces = []
    piece_checks = []
    for distance in range(-reach_devices, reach_devices + 1):
        if distance == 0:
            pieces.append(vectors)
            piece_checks.append(checks)
        else:
            shifted, shifted_check = shifted_2((vectors, checks), ("row", "col"), -distance)
            pieces.append(shifted)
            piece_checks.append(shifted_check)
    return (jnp.concatenate(pieces, 0), jnp.concatenate(piece_checks, 0))


def rows_split(start_vectors, ham_blocks, block_cols, block_counts, check_weights):
    row_vectors = lax.all_to_all(start_vectors, "col", split_axis=0, concat_axis=1, tiled=True)
    checks = jnp.dot(
        row_vectors, check_weights, precision=HIGHEST_PRECISION, preferred_element_type=jnp.float32
    )
    blocks_here = ham_blocks.shape[0]
    total_blocks = lax.axis_size(("row", "col")) * blocks_here
    position = lax.axis_index(("row", "col"))
    neighbours = (REACH + blocks_here - 1) // blocks_here
    base_block = (position - neighbours) * blocks_here

    def apply_operator(vectors, vector_checks):
        window, window_check = near_window(vectors, vector_checks, neighbours)
        return accumulate(
            ham_blocks, block_cols, block_counts, window, window_check, base_block, total_blocks
        )

    previous, previous_check = (row_vectors, checks)
    image_rows, image_check = apply_operator(row_vectors, checks)
    current = (image_rows - CENTRE * row_vectors) / HALF_WIDTH
    current_check = (image_check - CENTRE * checks) / HALF_WIDTH
    for step_index in range(ITERS - 1):
        image_rows, image_check = apply_operator(current, current_check)
        following = 2.0 * (image_rows - CENTRE * current) / HALF_WIDTH - previous
        following_check = 2.0 * (image_check - CENTRE * current_check) / HALF_WIDTH - previous_check
        previous, previous_check = (current, current_check)
        current, current_check = (following, following_check)
    filtered = lax.all_to_all(current, "col", split_axis=1, concat_axis=0, tiled=True)
    return (filtered, current_check)


def split2(x):
    high = x.astype(jnp.bfloat16)
    low = (x - high.astype(jnp.float32)).astype(jnp.bfloat16)
    return high, low


def beyond(count, slot):
    return jnp.minimum(jnp.maximum(count - slot, 0), 1)


def filter_kernel(
    rows_n, v_hbm, h_ref, cols_ref, counts_ref, colsh_ref, countsh_ref, w_hbm, out_ref, chk_ref,
    v_ref, w_ref, hv, hr, st, es, em, ex, ec, er, colsp, countsp, a_ref, ea_ref, win, p_ref, y1, y2,
    halo, cs_s, cs_r, send, recv, loc,
):
    r = lax.axis_index("row")
    y = lax.axis_index("col")
    right, left = lax.rem(r + 1, rows_n), lax.rem(r + rows_n - 1, rows_n)
    core = lax.rem(r, 2)
    pair = lax.rem(r // 2, 2)
    blocks, cap, size, _ = hv.shape
    group = 2 * blocks
    total = rows_n * group
    heavy_slots = cap - LIGHT
    half_rows = blocks // 2
    peer = {"col": 1 - y}
    sibling = {"row": r + 1 - 2 * core}
    across = {"row": r + 2 - 4 * pair}

    barrier = pltpu.get_barrier_semaphore()
    for target in ({"row": left}, {"row": right}, across, peer):
        pl.semaphore_signal(barrier, inc=1, device_id=target, device_id_type=MESH)

    own_copy = pltpu.make_async_copy(h_ref, hv, loc.at[0])
    vector_copy = pltpu.make_async_copy(v_hbm, v_ref, loc.at[1])
    weight_copy = pltpu.make_async_copy(w_hbm, w_ref, loc.at[2])
    own_copy.start()
    vector_copy.start()
    weight_copy.start()
    pl.semaphore_wait(barrier, 4)

    def remote(src, dst, index, target):
        return pltpu.make_async_remote_copy(
            src_ref=src, dst_ref=dst, send_sem=send.at[index], recv_sem=recv.at[index],
            device_id=target, device_id_type=MESH,
        )

    mine_row = half_rows * core + pair
    other_row = half_rows * core + 1 - pair
    cols_copy = remote(colsh_ref, colsp, 0, peer)
    counts_copy = remote(countsh_ref, countsp, 1, peer)

    def light_part(part, first_row, count):
        at = pl.ds(first_row, count)
        return remote(h_ref.at[at, pl.ds(0, LIGHT)], hr.at[at], 2 + part, peer)

    lead = blocks - 1
    light_copies = (light_part(0, 0, lead), light_part(1, lead, 1))
    chip_copy = remote(st, es, 4, sibling)
    pieces = 2
    piece = size // pieces

    def pieced(src, dst, index, target):
        copies = []
        for k in range(pieces):
            at = pl.ds(k * piece, piece)
            copies.append(remote(src.at[:, at], dst.at[:, at], index + k, target))
        return copies

    pair_copies = pieced(em.at[1 - pair], ex, 5, across)
    cross_copies = pieced(ec, er.at[mine_row], 7, peer)
    pair_shares = pieced(er.at[mine_row], er.at[mine_row], 9, across)
    chip_shares = pieced(er.at[mine_row], er.at[mine_row], 11, sibling)
    chip_shares_2 = pieced(er.at[other_row], er.at[other_row], 13, sibling)
    check_copy = remote(cs_s, cs_r, 15, peer)

    def halo_copies(source, step):
        own_rows = group * size
        to_right = remote(
            source.at[pl.ds(own_rows - REACH * size, REACH * size)],
            halo.at[step, pl.ds(0, REACH * size)], 16 + 2 * step, {"row": right},
        )
        to_left = remote(
            source.at[pl.ds(0, RIGHT_REACH * size)],
            halo.at[step, pl.ds(REACH * size, RIGHT_REACH * size)], 17 + 2 * step, {"row": left},
        )
        return to_right, to_left

    cols_copy.start()
    counts_copy.start()
    light_copies[0].start()

    def loop(count, body):
        def one(i, carry):
            body(i)
            return carry

        lax.fori_loop(0, count, one, 0, unroll=True)

    def put_window(source, src_at, dst_at, count):
        def one(i):
            at = pl.multiple_of(src_at + i * size, size)
            high, low = split2(source[pl.ds(at, size), :])
            win[dst_at + i, :, pl.ds(0, size)] = high
            win[dst_at + i, :, pl.ds(size, size)] = low

        loop(count, one)

    def put_halo(step):
        put_window(halo.at[step], 0, 0, REACH)
        put_window(halo.at[step], REACH * size, REACH + group, RIGHT_REACH)

    own_is_heavy = beyond(counts_ref[0, 0], LIGHT)
    own_heavy = own_is_heavy.astype(jnp.float32)

    own_copy.wait()

    def stage(i):
        st[i] = hv[half_rows * (1 - core) + i, pl.ds(LIGHT, heavy_slots)] * own_heavy

    loop(half_rows, stage)
    chip_copy.start()

    def put_light(source, table, half, first_row, count):
        def one(i):
            i = first_row + i
            live_count = table[0, i]
            for j in range(LIGHT):
                live = beyond(live_count, j).astype(jnp.float32)
                high, low = split2(source[i, j] * live)
                a_ref[half * blocks + i, pl.ds(0, size), pl.ds(j * size, size)] = high
                a_ref[half * blocks + i, pl.ds(size, size), pl.ds(j * size, size)] = low

        loop(count, one)

    def put_heavy(with_peer):
        def one(i):
            for j in range(heavy_slots):
                live = beyond(counts_ref[0, i], LIGHT + j).astype(jnp.float32)
                value = hv[i, LIGHT + j] * live
                if with_peer:
                    live = beyond(countsp[0, i], LIGHT + j).astype(jnp.float32) * (1.0 - own_heavy)
                    value = value + er[i, j] * live
                high, low = split2(value)
                ea_ref[i, pl.ds(0, size), pl.ds(j * size, size)] = high
                ea_ref[i, pl.ds(size, size), pl.ds(j * size, size)] = low

        loop(blocks, one)

    put_light(hv, counts_ref, y, 0, blocks)
    chip_copy.wait_recv()

    def merge(i):
        em[i] = hv[half_rows * core + i, pl.ds(LIGHT, heavy_slots)] * own_heavy + es[i]

    loop(half_rows, merge)
    for copy in pair_copies:
        copy.start()

    put_heavy(False)
    vector_copy.wait()
    put_window(v_ref, 0, REACH, group)
    cols_copy.wait_recv()
    counts_copy.wait_recv()
    peer_heavy = beyond(countsp[0, 0], LIGHT).astype(jnp.float32)

    for k in range(pieces):
        pair_copies[k].wait_recv()
        at = pl.ds(k * piece, piece)
        ec[:, at, :] = em[pair, :, at, :] + ex[:, at, :]
        cross_copies[k].start()
    first = halo_copies(v_hbm, 0)
    first[0].start()
    first[1].start()

    base = r * group - REACH + total

    def tile(col):
        return win[jnp.minimum(lax.rem(col - base + 2 * total, total), win.shape[0] - 1)]

    def product(matrix, cols):
        tiles = jnp.concatenate([tile(col) for col in cols], 0)
        full = jnp.dot(matrix, tiles, preferred_element_type=jnp.float32)
        big = full[:size, :size]
        small = full[:size, size:] + full[size:, :size] + full[size:, size:]
        return big + small

    def heavy_products():
        def one(i):
            cols = []
            for j in range(LIGHT, cap):
                own_col, peer_col = cols_ref[i, j], colsp[i, j]
                cols.append(peer_col + own_is_heavy * (own_col - peer_col))
            p_ref[i] = product(ea_ref[i], cols)

        loop(blocks, one)

    def place(half, i):
        return pl.ds(pl.multiple_of((half * blocks + i) * size, size), size)

    def rows(half, source, older, target, first_row=0, count=blocks, heavy=True):
        mine = y * half + (1 - y) * (1 - half)
        share = mine.astype(jnp.float32)
        flag = own_heavy * share + peer_heavy * (1.0 - share)

        def one(i):
            i = first_row + i
            cols = []
            for j in range(LIGHT):
                own_col, peer_col = cols_ref[i, j], colsp[i, j]
                cols.append(peer_col + mine * (own_col - peer_col))
            image = product(a_ref[half * blocks + i], cols)
            if heavy:
                image = image + p_ref[i] * flag
            at = place(half, i)
            value = (image - CENTRE * source[at, :]) * (1.0 / HALF_WIDTH)
            if older is not None:
                value = 2.0 * value - older[at, :]
            target[at, :] = value

        loop(count, one)

    def share(k):
        cross_copies[k].wait_recv()
        pair_shares[k].start()
        chip_shares[k].start()

    share(0)
    first[0].wait_recv()
    first[1].wait_recv()
    put_halo(0)
    heavy_products()
    rows(y, v_ref, None, y1)
    share(1)
    for copy in cross_copies:
        copy.wait_send()
    light_copies[1].start()
    second = halo_copies(y1, 1)

    def send_halo(half, copies):
        @pl.when(half == 1)
        def _():
            copies[0].start()

        @pl.when(half == 0)
        def _():
            copies[1].start()

    send_halo(y, second)
    light_copies[0].wait_recv()
    put_light(hr, countsp, 1 - y, 0, lead)
    rows(1 - y, v_ref, None, y1, 0, lead, False)
    for k in range(pieces):
        pair_shares[k].wait_recv()
        chip_shares_2[k].start()
    for copy in (*chip_shares, *chip_shares_2):
        copy.wait_recv()
    put_heavy(True)
    heavy_products()

    def add_heavy(i):
        at = place(1 - y, i)
        y1[at, :] = y1[at, :] + p_ref[i] * (peer_heavy * (1.0 / HALF_WIDTH))

    loop(lead, add_heavy)
    light_copies[1].wait_recv()
    put_light(hr, countsp, 1 - y, lead, 1)
    rows(1 - y, v_ref, None, y1, lead, 1)
    send_halo(1 - y, second)

    def take_halo(half, copies, step):
        @pl.when(half == 0)
        def _():
            copies[0].wait_recv()
            put_window(halo.at[step], 0, 0, REACH)

        @pl.when(half == 1)
        def _():
            copies[1].wait_recv()
            put_window(halo.at[step], REACH * size, REACH + group, RIGHT_REACH)

    chain = ((v_ref, None, y1), (y1, v_ref, y2), (y2, y1, out_ref))
    started = [*first, *second]
    early, late = 1 - y, y
    for step in range(1, ITERS):
        source, older, target = chain[step]
        copies = started[2 * step:]
        following = halo_copies(target, step + 1) if step < ITERS - 1 else ()
        started += following
        put_window(source, 0, REACH, group)
        for half in (early, late):
            take_halo(half, copies, step)
            heavy_products()
            rows(half, source, older, target)
            if following:
                send_halo(half, following)
        early, late = late, early

    weight_copy.wait()
    weights = jnp.where(y == 0, w_ref[:, :size], w_ref[:, size:])
    w_high, w_rest = split2(weights)
    w_low = (weights - w_high.astype(jnp.float32) - w_rest.astype(jnp.float32)).astype(jnp.bfloat16)
    w_parts = jnp.concatenate([w_high, w_rest, w_low, jnp.zeros((13, size), jnp.bfloat16)], 0)

    def partial(half):
        at = pl.ds(pl.multiple_of(half * blocks * size, size), blocks * size)
        total_dot = 0.0
        for part in split2(out_ref[at, :]):
            total_dot += lax.dot_general(
                w_parts, part, (((1,), (1,)), ((), ())), preferred_element_type=jnp.float32
            )
        return jnp.sum(total_dot, 0, keepdims=True)

    cs_s[...] = partial(1 - y)
    check_copy.start()
    own_part = partial(y)
    check_copy.wait_recv()
    chk_ref[...] = own_part + cs_r[...]

    for copy in (
        cols_copy, counts_copy, *light_copies, chip_copy, *pair_copies, *pair_shares, *chip_shares,
        *chip_shares_2, check_copy, *started,
    ):
        copy.wait_send()


def columns_split(start_vectors, ham_blocks, block_cols, block_counts, check_weights):
    blocks, cap, size, _ = ham_blocks.shape
    rows_n = lax.axis_size("row")
    group = 2 * blocks
    height, width = start_vectors.shape
    counts = block_counts.reshape(1, blocks)
    window = REACH + group + RIGHT_REACH
    f32, bf16 = jnp.float32, jnp.bfloat16
    heavy = cap - LIGHT
    vmem = pl.BlockSpec(memory_space=pltpu.VMEM)
    smem = pl.BlockSpec(memory_space=pltpu.SMEM)
    anywhere = pl.BlockSpec(memory_space=pl.ANY)
    filtered, check = pl.pallas_call(
        functools.partial(filter_kernel, rows_n),
        out_shape=(
            jax.ShapeDtypeStruct((height, width), f32),
            jax.ShapeDtypeStruct((1, blocks * size), f32),
        ),
        in_specs=[anywhere, anywhere, smem, smem, anywhere, anywhere, anywhere],
        out_specs=(vmem, vmem),
        scratch_shapes=[
            pltpu.VMEM((height, width), f32),
            pltpu.VMEM((1, 2 * width), f32),
            pltpu.VMEM((blocks, cap, size, size), f32),
            pltpu.VMEM((blocks, LIGHT, size, size), f32),
            pltpu.VMEM((blocks // 2, heavy, size, size), f32),
            pltpu.VMEM((blocks // 2, heavy, size, size), f32),
            pltpu.VMEM((blocks // 2, heavy, size, size), f32),
            pltpu.VMEM((heavy, size, size), f32),
            pltpu.VMEM((heavy, size, size), f32),
            pltpu.VMEM((blocks, heavy, size, size), f32),
            pltpu.SMEM((blocks, cap), jnp.int32),
            pltpu.SMEM((1, blocks), jnp.int32),
            pltpu.VMEM((group, 2 * size, LIGHT * size), bf16),
            pltpu.VMEM((blocks, 2 * size, heavy * size), bf16),
            pltpu.VMEM((window, size, 2 * width), bf16),
            pltpu.VMEM((blocks, size, width), f32),
            pltpu.VMEM((height, width), f32),
            pltpu.VMEM((height, width), f32),
            pltpu.VMEM((ITERS, (REACH + RIGHT_REACH) * size, width), f32),
            pltpu.VMEM((1, blocks * size), f32),
            pltpu.VMEM((1, blocks * size), f32),
            pltpu.SemaphoreType.DMA((16 + 2 * ITERS,)),
            pltpu.SemaphoreType.DMA((16 + 2 * ITERS,)),
            pltpu.SemaphoreType.DMA((3,)),
        ],
        compiler_params=pltpu.CompilerParams(
            collective_id=0, has_side_effects=True, vmem_limit_bytes=60 * 1024 * 1024
        ),
    )(start_vectors, ham_blocks, block_cols, counts, block_cols, counts, check_weights.reshape(1, -1))
    return (filtered, check.reshape(-1))


def solution(mesh):
    placed = (
        P("row", "col"),
        P(("row", "col"), None, None, None),
        P(("row", "col"), None),
        P(("row", "col")),
        P(),
    )
    devices = mesh.shape["row"] * mesh.shape["col"]
    one_heavy = devices < 64 and mesh.shape["col"] == 2 and mesh.shape["row"] >= 8 and mesh.shape["row"] % 4 == 0
    return jax.shard_map(
        columns_split if one_heavy else rows_split,
        mesh=mesh,
        in_specs=placed,
        out_specs=(P("row", "col"), P(("row", "col"))),
        check_vma=False,
    )
```

```python
import functools

import jax
import jax.numpy as jnp
from jax import lax
from jax.experimental import pallas as pl
from jax.experimental.pallas import tpu as pltpu
from jax.sharding import PartitionSpec as P

REACH = 4
RIGHT_REACH = 3
LIGHT = 3
ITERS = 3


CENTRE = 0.25
HALF_WIDTH = 1.5
HIGHEST_PRECISION = lax.Precision.HIGHEST
MESH = pl.DeviceIdType.MESH


def shifted_2(value, axis, steps):
    count = lax.axis_size(axis)
    pairs = [(source, (source + steps) % count) for source in range(count)]
    return lax.ppermute(value, axis, pairs)


def accumulate(ham_blocks, block_cols, finishes, window, window_check, base_block, total_blocks):
    block_size = ham_blocks.shape[2]
    vector_width = window.shape[1]
    results = []
    result_checks = []
    for row_index in range(ham_blocks.shape[0]):
        matrices = ham_blocks[row_index]
        columns = block_cols[row_index]

        def add_block(slot_index, carried, matrices=matrices, columns=columns):
            summed, summed_check = carried
            offset = jnp.mod(columns[slot_index] - base_block, total_blocks) * block_size
            segment = lax.dynamic_slice_in_dim(window, offset, block_size, 0)
            segment_check = lax.dynamic_slice_in_dim(window_check, offset, block_size, 0)
            matrix = lax.dynamic_index_in_dim(matrices, slot_index, 0, keepdims=False)
            summed = summed + jnp.dot(
                matrix, segment, precision=HIGHEST_PRECISION, preferred_element_type=jnp.float32
            )
            summed_check = summed_check + jnp.dot(
                matrix,
                segment_check,
                precision=HIGHEST_PRECISION,
                preferred_element_type=jnp.float32,
            )
            return (summed, summed_check)

        initial = (
            jnp.zeros((block_size, vector_width), jnp.float32),
            jnp.zeros((block_size,), jnp.float32),
        )
        summed, summed_check = lax.fori_loop(0, finishes[row_index], add_block, initial)
        results.append(summed)
        result_checks.append(summed_check)
    return (jnp.concatenate(results, 0), jnp.concatenate(result_checks, 0))


def near_window(vectors, checks, reach_devices):
    pieces = []
    piece_checks = []
    for distance in range(-reach_devices, reach_devices + 1):
        if distance == 0:
            pieces.append(vectors)
            piece_checks.append(checks)
        else:
            shifted, shifted_check = shifted_2((vectors, checks), ("row", "col"), -distance)
            pieces.append(shifted)
            piece_checks.append(shifted_check)
    return (jnp.concatenate(pieces, 0), jnp.concatenate(piece_checks, 0))


def rows_split(start_vectors, ham_blocks, block_cols, block_counts, check_weights):
    row_vectors = lax.all_to_all(start_vectors, "col", split_axis=0, concat_axis=1, tiled=True)
    checks = jnp.dot(
        row_vectors, check_weights, precision=HIGHEST_PRECISION, preferred_element_type=jnp.float32
    )
    blocks_here = ham_blocks.shape[0]
    total_blocks = lax.axis_size(("row", "col")) * blocks_here
    position = lax.axis_index(("row", "col"))
    neighbours = (REACH + blocks_here - 1) // blocks_here
    base_block = (position - neighbours) * blocks_here

    def apply_operator(vectors, vector_checks):
        window, window_check = near_window(vectors, vector_checks, neighbours)
        return accumulate(
            ham_blocks, block_cols, block_counts, window, window_check, base_block, total_blocks
        )

    previous, previous_check = (row_vectors, checks)
    image_rows, image_check = apply_operator(row_vectors, checks)
    current = (image_rows - CENTRE * row_vectors) / HALF_WIDTH
    current_check = (image_check - CENTRE * checks) / HALF_WIDTH
    for step_index in range(ITERS - 1):
        image_rows, image_check = apply_operator(current, current_check)
        following = 2.0 * (image_rows - CENTRE * current) / HALF_WIDTH - previous
        following_check = 2.0 * (image_check - CENTRE * current_check) / HALF_WIDTH - previous_check
        previous, previous_check = (current, current_check)
        current, current_check = (following, following_check)
    filtered = lax.all_to_all(current, "col", split_axis=1, concat_axis=0, tiled=True)
    return (filtered, current_check)


def split2(x):
    high = x.astype(jnp.bfloat16)
    low = (x - high.astype(jnp.float32)).astype(jnp.bfloat16)
    return high, low


def beyond(count, slot):
    return jnp.minimum(jnp.maximum(count - slot, 0), 1)


def filter_kernel(
    rows_n, v_hbm, h_ref, cols_ref, counts_ref, colsh_ref, countsh_ref, w_hbm, out_ref, chk_ref,
    v_ref, w_ref, hv, hr, st, es, em, ex, ec, er, colsp, countsp, a_ref, win, y1, y2,
    halo, cs_s, cs_r, send, recv, loc,
):
    r = lax.axis_index("row")
    y = lax.axis_index("col")
    right, left = lax.rem(r + 1, rows_n), lax.rem(r + rows_n - 1, rows_n)
    core = lax.rem(r, 2)
    sides = (lax.rem(r // 2, 2), lax.rem(r // 4, 2))
    blocks, cap, size, _ = hv.shape
    group = 2 * blocks
    total = rows_n * group
    heavy_slots = cap - LIGHT
    half_rows = blocks // 2
    peer = {"col": 1 - y}
    sibling = {"row": r + 1 - 2 * core}
    across = ({"row": r + 2 - 4 * sides[0]}, {"row": r + 4 - 8 * sides[1]})

    barrier = pltpu.get_barrier_semaphore()
    for target in ({"row": left}, {"row": right}, *across, peer):
        pl.semaphore_signal(barrier, inc=1, device_id=target, device_id_type=MESH)

    own_copy = pltpu.make_async_copy(h_ref, hv, loc.at[0])
    vector_copy = pltpu.make_async_copy(v_hbm, v_ref, loc.at[1])
    weight_copy = pltpu.make_async_copy(w_hbm, w_ref, loc.at[2])
    own_copy.start()
    vector_copy.start()
    weight_copy.start()
    pl.semaphore_wait(barrier, 5)

    def remote(src, dst, index, target):
        return pltpu.make_async_remote_copy(
            src_ref=src, dst_ref=dst, send_sem=send.at[index], recv_sem=recv.at[index],
            device_id=target, device_id_type=MESH,
        )

    mine_rows = [half_rows * core + side for side in sides]
    other_rows = [half_rows * core + 1 - side for side in sides]
    cols_copy = remote(colsh_ref, colsp, 0, peer)
    counts_copy = remote(countsh_ref, countsp, 1, peer)

    def light_part(part, first_row, count):
        at = pl.ds(first_row, count)
        return remote(h_ref.at[at, pl.ds(0, LIGHT)], hr.at[at], 2 + part, peer)

    lead = blocks - 1
    light_copies = (light_part(0, 0, lead), light_part(1, lead, 1))
    chip_copy = remote(st, es, 4, sibling)
    pieces = len(sides)
    piece = size // pieces
    spans = [pl.ds(k * piece, piece) for k in range(pieces)]

    def shares(rows_of, index, targets):
        copies = []
        for k in range(pieces):
            part = er.at[rows_of[k], :, spans[k]]
            copies.append(remote(part, part, index + k, targets[k]))
        return copies

    pair_copies = [
        remote(em.at[1 - sides[k], :, spans[k]], ex.at[:, spans[k]], 5 + k, across[k]) for k in range(pieces)
    ]
    cross_copies = [
        remote(ec.at[:, spans[k]], er.at[mine_rows[k], :, spans[k]], 7 + k, peer) for k in range(pieces)
    ]
    pair_shares = shares(mine_rows, 9, across)
    chip_shares = shares(mine_rows, 11, [sibling] * pieces)
    chip_shares_2 = shares(other_rows, 13, [sibling] * pieces)
    check_copy = remote(cs_s, cs_r, 15, peer)

    def halo_copies(source, step):
        own_rows = group * size
        to_right = remote(
            source.at[pl.ds(own_rows - REACH * size, REACH * size)],
            halo.at[step, pl.ds(0, REACH * size)], 16 + 2 * step, {"row": right},
        )
        to_left = remote(
            source.at[pl.ds(0, RIGHT_REACH * size)],
            halo.at[step, pl.ds(REACH * size, RIGHT_REACH * size)], 17 + 2 * step, {"row": left},
        )
        return to_right, to_left

    cols_copy.start()
    counts_copy.start()
    light_copies[0].start()

    def loop(count, body):
        def one(i, carry):
            body(i)
            return carry

        lax.fori_loop(0, count, one, 0, unroll=True)

    def put_window(source, src_at, dst_at, count):
        def one(i):
            at = pl.multiple_of(src_at + i * size, size)
            high, low = split2(source[pl.ds(at, size), :])
            win[dst_at + i, :, pl.ds(0, size)] = high
            win[dst_at + i, :, pl.ds(size, size)] = low

        loop(count, one)

    def put_halo(step):
        put_window(halo.at[step], 0, 0, REACH)
        put_window(halo.at[step], REACH * size, REACH + group, RIGHT_REACH)

    own_heavy = beyond(counts_ref[0, 0], LIGHT).astype(jnp.float32)

    own_copy.wait()

    def stage(i):
        st[i] = hv[half_rows * (1 - core) + i, pl.ds(LIGHT, heavy_slots)] * own_heavy

    loop(half_rows, stage)
    chip_copy.start()

    def put_slots(source, source_slot, table, half, first_row, count, slots):
        def one(i):
            i = first_row + i
            live_count = table[0, i]
            for j in slots:
                live = beyond(live_count, j).astype(jnp.float32)
                high, low = split2(source[i, j - source_slot] * live)
                a_ref[half * blocks + i, pl.ds(0, size), pl.ds(j * size, size)] = high
                a_ref[half * blocks + i, pl.ds(size, size), pl.ds(j * size, size)] = low

        loop(count, one)

    light_slots, more_slots, all_slots = range(LIGHT), range(LIGHT, cap), range(cap)
    put_slots(hv, 0, counts_ref, y, 0, blocks, light_slots)
    chip_copy.wait_recv()

    def merge(i):
        em[i] = hv[half_rows * core + i, pl.ds(LIGHT, heavy_slots)] * own_heavy + es[i]

    loop(half_rows, merge)
    for copy in pair_copies:
        copy.start()

    put_slots(hv, 0, counts_ref, y, 0, blocks, more_slots)
    vector_copy.wait()
    put_window(v_ref, 0, REACH, group)
    cols_copy.wait_recv()
    counts_copy.wait_recv()

    for k in range(pieces):
        pair_copies[k].wait_recv()
        at = spans[k]
        ec[:, at, :] = em[sides[k], :, at, :] + ex[:, at, :]
        cross_copies[k].start()
    first = halo_copies(v_hbm, 0)
    first[0].start()
    first[1].start()

    base = r * group - REACH + total

    def tile(col):
        return win[jnp.minimum(lax.rem(col - base + 2 * total, total), win.shape[0] - 1)]

    def product(matrix, cols):
        tiles = jnp.concatenate([tile(col) for col in cols], 0)
        full = jnp.dot(matrix, tiles, preferred_element_type=jnp.float32)
        big = full[:size, :size]
        small = full[:size, size:] + full[size:, :size] + full[size:, size:]
        return big + small

    def place(half, i):
        return pl.ds(pl.multiple_of((half * blocks + i) * size, size), size)

    def image_of(half, i, slots):
        mine = y * half + (1 - y) * (1 - half)
        cols = []
        for j in slots:
            own_col, peer_col = cols_ref[i, j], colsp[i, j]
            cols.append(peer_col + mine * (own_col - peer_col))
        lanes = pl.ds(slots[0] * size, len(slots) * size)
        return product(a_ref[half * blocks + i, :, lanes], cols)

    def rows(half, source, older, target, first_row=0, count=blocks, slots=all_slots):
        def one(i):
            i = first_row + i
            image = image_of(half, i, slots)
            at = place(half, i)
            value = (image - CENTRE * source[at, :]) * (1.0 / HALF_WIDTH)
            if older is not None:
                value = 2.0 * value - older[at, :]
            target[at, :] = value

        loop(count, one)

    def share(k):
        cross_copies[k].wait_recv()
        pair_shares[k].start()
        chip_shares[k].start()

    share(0)
    first[0].wait_recv()
    first[1].wait_recv()
    put_halo(0)
    rows(y, v_ref, None, y1)
    share(1)
    for copy in cross_copies:
        copy.wait_send()
    light_copies[1].start()
    second = halo_copies(y1, 1)

    def send_halo(half, copies):
        @pl.when(half == 1)
        def _():
            copies[0].start()

        @pl.when(half == 0)
        def _():
            copies[1].start()

    send_halo(y, second)
    light_copies[0].wait_recv()
    put_slots(hr, 0, countsp, 1 - y, 0, lead, light_slots)
    rows(1 - y, v_ref, None, y1, 0, lead, light_slots)
    for k in range(pieces):
        pair_shares[k].wait_recv()
        chip_shares_2[k].start()
    for copy in (*chip_shares, *chip_shares_2):
        copy.wait_recv()
    put_slots(er, LIGHT, countsp, 1 - y, 0, blocks, more_slots)

    def add_heavy(i):
        at = place(1 - y, i)
        y1[at, :] = y1[at, :] + image_of(1 - y, i, more_slots) * (1.0 / HALF_WIDTH)

    loop(lead, add_heavy)
    light_copies[1].wait_recv()
    put_slots(hr, 0, countsp, 1 - y, lead, 1, light_slots)
    rows(1 - y, v_ref, None, y1, lead, 1)
    send_halo(1 - y, second)

    def take_halo(half, copies, step):
        @pl.when(half == 0)
        def _():
            copies[0].wait_recv()
            put_window(halo.at[step], 0, 0, REACH)

        @pl.when(half == 1)
        def _():
            copies[1].wait_recv()
            put_window(halo.at[step], REACH * size, REACH + group, RIGHT_REACH)

    chain = ((v_ref, None, y1), (y1, v_ref, y2), (y2, y1, out_ref))
    started = [*first, *second]
    early, late = 1 - y, y
    for step in range(1, ITERS):
        source, older, target = chain[step]
        copies = started[2 * step:]
        following = halo_copies(target, step + 1) if step < ITERS - 1 else ()
        started += following
        put_window(source, 0, REACH, group)
        for half in (early, late):
            take_halo(half, copies, step)
            rows(half, source, older, target)
            if following:
                send_halo(half, following)
        early, late = late, early

    weight_copy.wait()
    weights = jnp.where(y == 0, w_ref[:, :size], w_ref[:, size:])
    w_high, w_rest = split2(weights)
    w_low = (weights - w_high.astype(jnp.float32) - w_rest.astype(jnp.float32)).astype(jnp.bfloat16)
    w_parts = jnp.concatenate([w_high, w_rest, w_low, jnp.zeros((13, size), jnp.bfloat16)], 0)

    def partial(half):
        at = pl.ds(pl.multiple_of(half * blocks * size, size), blocks * size)
        total_dot = 0.0
        for part in split2(out_ref[at, :]):
            total_dot += lax.dot_general(
                w_parts, part, (((1,), (1,)), ((), ())), preferred_element_type=jnp.float32
            )
        return jnp.sum(total_dot, 0, keepdims=True)

    cs_s[...] = partial(1 - y)
    check_copy.start()
    own_part = partial(y)
    check_copy.wait_recv()
    chk_ref[...] = own_part + cs_r[...]

    for copy in (
        cols_copy, counts_copy, *light_copies, chip_copy, *pair_copies, *pair_shares, *chip_shares,
        *chip_shares_2, check_copy, *started,
    ):
        copy.wait_send()


def columns_split(start_vectors, ham_blocks, block_cols, block_counts, check_weights):
    blocks, cap, size, _ = ham_blocks.shape
    rows_n = lax.axis_size("row")
    group = 2 * blocks
    height, width = start_vectors.shape
    counts = block_counts.reshape(1, blocks)
    window = REACH + group + RIGHT_REACH
    f32, bf16 = jnp.float32, jnp.bfloat16
    heavy = cap - LIGHT
    vmem = pl.BlockSpec(memory_space=pltpu.VMEM)
    smem = pl.BlockSpec(memory_space=pltpu.SMEM)
    anywhere = pl.BlockSpec(memory_space=pl.ANY)
    filtered, check = pl.pallas_call(
        functools.partial(filter_kernel, rows_n),
        out_shape=(
            jax.ShapeDtypeStruct((height, width), f32),
            jax.ShapeDtypeStruct((1, blocks * size), f32),
        ),
        in_specs=[anywhere, anywhere, smem, smem, anywhere, anywhere, anywhere],
        out_specs=(vmem, vmem),
        scratch_shapes=[
            pltpu.VMEM((height, width), f32),
            pltpu.VMEM((1, 2 * width), f32),
            pltpu.VMEM((blocks, cap, size, size), f32),
            pltpu.VMEM((blocks, LIGHT, size, size), f32),
            pltpu.VMEM((blocks // 2, heavy, size, size), f32),
            pltpu.VMEM((blocks // 2, heavy, size, size), f32),
            pltpu.VMEM((blocks // 2, heavy, size, size), f32),
            pltpu.VMEM((heavy, size, size), f32),
            pltpu.VMEM((heavy, size, size), f32),
            pltpu.VMEM((blocks, heavy, size, size), f32),
            pltpu.SMEM((blocks, cap), jnp.int32),
            pltpu.SMEM((1, blocks), jnp.int32),
            pltpu.VMEM((group, 2 * size, cap * size), bf16),
            pltpu.VMEM((window, size, 2 * width), bf16),
            pltpu.VMEM((height, width), f32),
            pltpu.VMEM((height, width), f32),
            pltpu.VMEM((ITERS, (REACH + RIGHT_REACH) * size, width), f32),
            pltpu.VMEM((1, blocks * size), f32),
            pltpu.VMEM((1, blocks * size), f32),
            pltpu.SemaphoreType.DMA((16 + 2 * ITERS,)),
            pltpu.SemaphoreType.DMA((16 + 2 * ITERS,)),
            pltpu.SemaphoreType.DMA((3,)),
        ],
        compiler_params=pltpu.CompilerParams(
            collective_id=0, has_side_effects=True, vmem_limit_bytes=60 * 1024 * 1024
        ),
    )(start_vectors, ham_blocks, block_cols, counts, block_cols, counts, check_weights.reshape(1, -1))
    return (filtered, check.reshape(-1))


def solution(mesh):
    placed = (
        P("row", "col"),
        P(("row", "col"), None, None, None),
        P(("row", "col"), None),
        P(("row", "col")),
        P(),
    )
    devices = mesh.shape["row"] * mesh.shape["col"]
    one_heavy = devices < 64 and mesh.shape["col"] == 2 and mesh.shape["row"] >= 16 and mesh.shape["row"] % 8 == 0
    return jax.shard_map(
        columns_split if one_heavy else rows_split,
        mesh=mesh,
        in_specs=placed,
        out_specs=(P("row", "col"), P(("row", "col"))),
        check_vma=False,
    )
```

```python
import functools

import jax
import jax.numpy as jnp
from jax import lax
from jax.experimental import pallas as pl
from jax.experimental.pallas import tpu as pltpu
from jax.sharding import PartitionSpec as P

REACH = 4
RIGHT_REACH = 3
LIGHT = 3
ITERS = 3


CENTRE = 0.25
HALF_WIDTH = 1.5
HIGHEST_PRECISION = lax.Precision.HIGHEST
MESH = pl.DeviceIdType.MESH


def shifted_2(value, axis, steps):
    count = lax.axis_size(axis)
    pairs = [(source, (source + steps) % count) for source in range(count)]
    return lax.ppermute(value, axis, pairs)


def accumulate(ham_blocks, block_cols, finishes, window, window_check, base_block, total_blocks):
    block_size = ham_blocks.shape[2]
    vector_width = window.shape[1]
    results = []
    result_checks = []
    for row_index in range(ham_blocks.shape[0]):
        matrices = ham_blocks[row_index]
        columns = block_cols[row_index]

        def add_block(slot_index, carried, matrices=matrices, columns=columns):
            summed, summed_check = carried
            offset = jnp.mod(columns[slot_index] - base_block, total_blocks) * block_size
            segment = lax.dynamic_slice_in_dim(window, offset, block_size, 0)
            segment_check = lax.dynamic_slice_in_dim(window_check, offset, block_size, 0)
            matrix = lax.dynamic_index_in_dim(matrices, slot_index, 0, keepdims=False)
            summed = summed + jnp.dot(
                matrix, segment, precision=HIGHEST_PRECISION, preferred_element_type=jnp.float32
            )
            summed_check = summed_check + jnp.dot(
                matrix,
                segment_check,
                precision=HIGHEST_PRECISION,
                preferred_element_type=jnp.float32,
            )
            return (summed, summed_check)

        initial = (
            jnp.zeros((block_size, vector_width), jnp.float32),
            jnp.zeros((block_size,), jnp.float32),
        )
        summed, summed_check = lax.fori_loop(0, finishes[row_index], add_block, initial)
        results.append(summed)
        result_checks.append(summed_check)
    return (jnp.concatenate(results, 0), jnp.concatenate(result_checks, 0))


def near_window(vectors, checks, reach_devices):
    pieces = []
    piece_checks = []
    for distance in range(-reach_devices, reach_devices + 1):
        if distance == 0:
            pieces.append(vectors)
            piece_checks.append(checks)
        else:
            shifted, shifted_check = shifted_2((vectors, checks), ("row", "col"), -distance)
            pieces.append(shifted)
            piece_checks.append(shifted_check)
    return (jnp.concatenate(pieces, 0), jnp.concatenate(piece_checks, 0))


def rows_split(start_vectors, ham_blocks, block_cols, block_counts, check_weights):
    row_vectors = lax.all_to_all(start_vectors, "col", split_axis=0, concat_axis=1, tiled=True)
    checks = jnp.dot(
        row_vectors, check_weights, precision=HIGHEST_PRECISION, preferred_element_type=jnp.float32
    )
    blocks_here = ham_blocks.shape[0]
    total_blocks = lax.axis_size(("row", "col")) * blocks_here
    position = lax.axis_index(("row", "col"))
    neighbours = (REACH + blocks_here - 1) // blocks_here
    base_block = (position - neighbours) * blocks_here

    def apply_operator(vectors, vector_checks):
        window, window_check = near_window(vectors, vector_checks, neighbours)
        return accumulate(
            ham_blocks, block_cols, block_counts, window, window_check, base_block, total_blocks
        )

    previous, previous_check = (row_vectors, checks)
    image_rows, image_check = apply_operator(row_vectors, checks)
    current = (image_rows - CENTRE * row_vectors) / HALF_WIDTH
    current_check = (image_check - CENTRE * checks) / HALF_WIDTH
    for step_index in range(ITERS - 1):
        image_rows, image_check = apply_operator(current, current_check)
        following = 2.0 * (image_rows - CENTRE * current) / HALF_WIDTH - previous
        following_check = 2.0 * (image_check - CENTRE * current_check) / HALF_WIDTH - previous_check
        previous, previous_check = (current, current_check)
        current, current_check = (following, following_check)
    filtered = lax.all_to_all(current, "col", split_axis=1, concat_axis=0, tiled=True)
    return (filtered, current_check)


def split2(x):
    high = x.astype(jnp.bfloat16)
    low = (x - high.astype(jnp.float32)).astype(jnp.bfloat16)
    return high, low


def beyond(count, slot):
    return jnp.minimum(jnp.maximum(count - slot, 0), 1)


def filter_kernel(
    rows_n, v_hbm, h_ref, cols_ref, counts_ref, colsh_ref, countsh_ref, w_hbm, out_hbm, chk_ref,
    v_ref, w_ref, out_ref, hv, hr, st, es, em, ex, ec, er, colsp, countsp, a_ref, win, y1, y2,
    halo, cs_s, cs_r, send, recv, loc,
):
    r = lax.axis_index("row")
    y = lax.axis_index("col")
    right, left = lax.rem(r + 1, rows_n), lax.rem(r + rows_n - 1, rows_n)
    core = lax.rem(r, 2)
    sides = (lax.rem(r // 2, 2), lax.rem(r // 4, 2))
    blocks, cap, size, _ = hv.shape
    group = 2 * blocks
    total = rows_n * group
    heavy_slots = cap - LIGHT
    half_rows = blocks // 2
    peer = {"col": 1 - y}
    sibling = {"row": r + 1 - 2 * core}
    across = ({"row": r + 2 - 4 * sides[0]}, {"row": r + 4 - 8 * sides[1]})

    barrier = pltpu.get_barrier_semaphore()
    for target in ({"row": left}, {"row": right}, *across, peer):
        pl.semaphore_signal(barrier, inc=1, device_id=target, device_id_type=MESH)

    own_copy = pltpu.make_async_copy(h_ref, hv, loc.at[0])
    vector_copy = pltpu.make_async_copy(v_hbm, v_ref, loc.at[1])
    weight_copy = pltpu.make_async_copy(w_hbm, w_ref, loc.at[2])
    own_copy.start()
    vector_copy.start()
    weight_copy.start()
    pl.semaphore_wait(barrier, 5)

    def remote(src, dst, index, target):
        return pltpu.make_async_remote_copy(
            src_ref=src, dst_ref=dst, send_sem=send.at[index], recv_sem=recv.at[index],
            device_id=target, device_id_type=MESH,
        )

    mine_rows = [half_rows * core + side for side in sides]
    other_rows = [half_rows * core + 1 - side for side in sides]
    cols_copy = remote(colsh_ref, colsp, 0, peer)
    counts_copy = remote(countsh_ref, countsp, 1, peer)

    def light_part(part, first_row, count):
        at = pl.ds(first_row, count)
        return remote(h_ref.at[at, pl.ds(0, LIGHT)], hr.at[at], 2 + part, peer)

    lead = blocks - 1
    light_copies = (light_part(0, 0, lead), light_part(1, lead, 1))
    chip_copy = remote(st, es, 4, sibling)
    pieces = len(sides)
    piece = size // pieces
    spans = [pl.ds(k * piece, piece) for k in range(pieces)]

    def shares(rows_of, index, targets):
        copies = []
        for k in range(pieces):
            part = er.at[rows_of[k], :, spans[k]]
            copies.append(remote(part, part, index + k, targets[k]))
        return copies

    pair_copies = [
        remote(em.at[1 - sides[k], :, spans[k]], ex.at[:, spans[k]], 5 + k, across[k]) for k in range(pieces)
    ]
    cross_copies = [
        remote(ec.at[:, spans[k]], er.at[mine_rows[k], :, spans[k]], 7 + k, peer) for k in range(pieces)
    ]
    pair_shares = shares(mine_rows, 9, across)
    chip_shares = shares(mine_rows, 11, [sibling] * pieces)
    chip_shares_2 = shares(other_rows, 13, [sibling] * pieces)
    check_copy = remote(cs_s, cs_r, 15, peer)

    def halo_copies(source, step):
        own_rows = group * size
        to_right = remote(
            source.at[pl.ds(own_rows - REACH * size, REACH * size)],
            halo.at[step, pl.ds(0, REACH * size)], 16 + 2 * step, {"row": right},
        )
        to_left = remote(
            source.at[pl.ds(0, RIGHT_REACH * size)],
            halo.at[step, pl.ds(REACH * size, RIGHT_REACH * size)], 17 + 2 * step, {"row": left},
        )
        return to_right, to_left

    cols_copy.start()
    counts_copy.start()
    light_copies[0].start()

    def loop(count, body):
        def one(i, carry):
            body(i)
            return carry

        lax.fori_loop(0, count, one, 0, unroll=True)

    def put_window(source, src_at, dst_at, count):
        def one(i):
            at = pl.multiple_of(src_at + i * size, size)
            high, low = split2(source[pl.ds(at, size), :])
            win[dst_at + i, :, pl.ds(0, size)] = high
            win[dst_at + i, :, pl.ds(size, size)] = low

        loop(count, one)

    def put_halo(step):
        put_window(halo.at[step], 0, 0, REACH)
        put_window(halo.at[step], REACH * size, REACH + group, RIGHT_REACH)

    own_heavy = beyond(counts_ref[0, 0], LIGHT).astype(jnp.float32)

    own_copy.wait()

    def stage(i):
        st[i] = hv[half_rows * (1 - core) + i, pl.ds(LIGHT, heavy_slots)] * own_heavy

    loop(half_rows, stage)
    chip_copy.start()

    def put_slots(source, source_slot, table, half, first_row, count, slots):
        def one(i):
            i = first_row + i
            live_count = table[0, i]
            for j in slots:
                live = beyond(live_count, j).astype(jnp.float32)
                high, low = split2(source[i, j - source_slot] * live)
                a_ref[half * blocks + i, pl.ds(0, size), pl.ds(j * size, size)] = high
                a_ref[half * blocks + i, pl.ds(size, size), pl.ds(j * size, size)] = low

        loop(count, one)

    light_slots, more_slots, all_slots = range(LIGHT), range(LIGHT, cap), range(cap)
    put_slots(hv, 0, counts_ref, y, 0, blocks, light_slots)
    chip_copy.wait_recv()

    def merge(i):
        em[i] = hv[half_rows * core + i, pl.ds(LIGHT, heavy_slots)] * own_heavy + es[i]

    loop(half_rows, merge)
    for copy in pair_copies:
        copy.start()
    first = halo_copies(v_hbm, 0)
    first[0].start()
    first[1].start()

    put_slots(hv, 0, counts_ref, y, 0, blocks, more_slots)
    vector_copy.wait()
    put_window(v_ref, 0, REACH, group)
    cols_copy.wait_recv()
    counts_copy.wait_recv()

    for k in range(pieces):
        pair_copies[k].wait_recv()
        at = spans[k]
        ec[:, at, :] = em[sides[k], :, at, :] + ex[:, at, :]
        cross_copies[k].start()

    base = r * group - REACH + total

    def tile(col):
        return win[jnp.minimum(lax.rem(col - base + 2 * total, total), win.shape[0] - 1)]

    def product(matrix, cols):
        tiles = jnp.concatenate([tile(col) for col in cols], 0)
        full = jnp.dot(matrix, tiles, preferred_element_type=jnp.float32)
        big = full[:size, :size]
        small = full[:size, size:] + full[size:, :size] + full[size:, size:]
        return big + small

    def place(half, i):
        return pl.ds(pl.multiple_of((half * blocks + i) * size, size), size)

    def image_of(half, i, slots):
        mine = y * half + (1 - y) * (1 - half)
        cols = []
        for j in slots:
            own_col, peer_col = cols_ref[i, j], colsp[i, j]
            cols.append(peer_col + mine * (own_col - peer_col))
        lanes = pl.ds(slots[0] * size, len(slots) * size)
        return product(a_ref[half * blocks + i, :, lanes], cols)

    def rows(half, source, older, target, first_row=0, count=blocks, slots=all_slots):
        def one(i):
            i = first_row + i
            image = image_of(half, i, slots)
            at = place(half, i)
            value = (image - CENTRE * source[at, :]) * (1.0 / HALF_WIDTH)
            if older is not None:
                value = 2.0 * value - older[at, :]
            target[at, :] = value

        loop(count, one)

    def share(k):
        cross_copies[k].wait_recv()
        pair_shares[k].start()
        chip_shares[k].start()

    first[0].wait_recv()
    first[1].wait_recv()
    put_halo(0)
    rows(y, v_ref, None, y1)
    second = halo_copies(y1, 1)

    def send_halo(half, copies):
        @pl.when(half == 1)
        def _():
            copies[0].start()

        @pl.when(half == 0)
        def _():
            copies[1].start()

    send_halo(y, second)
    share(0)
    share(1)
    for copy in cross_copies:
        copy.wait_send()
    light_copies[1].start()
    light_copies[0].wait_recv()
    put_slots(hr, 0, countsp, 1 - y, 0, lead, light_slots)
    rows(1 - y, v_ref, None, y1, 0, lead, light_slots)
    for k in range(pieces):
        pair_shares[k].wait_recv()
        chip_shares_2[k].start()
    for copy in (*chip_shares, *chip_shares_2):
        copy.wait_recv()
    put_slots(er, LIGHT, countsp, 1 - y, 0, blocks, more_slots)

    def add_heavy(i):
        at = place(1 - y, i)
        y1[at, :] = y1[at, :] + image_of(1 - y, i, more_slots) * (1.0 / HALF_WIDTH)

    loop(lead, add_heavy)
    light_copies[1].wait_recv()
    put_slots(hr, 0, countsp, 1 - y, lead, 1, light_slots)
    rows(1 - y, v_ref, None, y1, lead, 1)
    send_halo(1 - y, second)

    def take_halo(half, copies, step):
        @pl.when(half == 0)
        def _():
            copies[0].wait_recv()
            put_window(halo.at[step], 0, 0, REACH)

        @pl.when(half == 1)
        def _():
            copies[1].wait_recv()
            put_window(halo.at[step], REACH * size, REACH + group, RIGHT_REACH)

    chain = ((v_ref, None, y1), (y1, v_ref, y2), (y2, y1, out_ref))
    started = [*first, *second]
    early, late = 1 - y, y
    out_copies = []
    for step in range(1, ITERS):
        source, older, target = chain[step]
        copies = started[2 * step:]
        following = halo_copies(target, step + 1) if step < ITERS - 1 else ()
        started += following
        put_window(source, 0, REACH, group)
        for half in (early, late):
            take_halo(half, copies, step)
            rows(half, source, older, target)
            if following:
                send_halo(half, following)
            else:
                at = pl.ds(pl.multiple_of(half * blocks * size, size), blocks * size)
                out_copies.append(pltpu.make_async_copy(out_ref.at[at], out_hbm.at[at], loc.at[3 + len(out_copies)]))
                out_copies[-1].start()
        early, late = late, early

    weight_copy.wait()
    weights = jnp.where(y == 0, w_ref[:, :size], w_ref[:, size:])
    w_high, w_rest = split2(weights)
    w_low = (weights - w_high.astype(jnp.float32) - w_rest.astype(jnp.float32)).astype(jnp.bfloat16)
    w_parts = jnp.concatenate([w_high, w_rest, w_low, jnp.zeros((13, size), jnp.bfloat16)], 0)

    def partial(half):
        at = pl.ds(pl.multiple_of(half * blocks * size, size), blocks * size)
        total_dot = 0.0
        for part in split2(out_ref[at, :]):
            total_dot += lax.dot_general(
                w_parts, part, (((1,), (1,)), ((), ())), preferred_element_type=jnp.float32
            )
        return jnp.sum(total_dot, 0, keepdims=True)

    cs_s[...] = partial(1 - y)
    check_copy.start()
    own_part = partial(y)
    check_copy.wait_recv()
    chk_ref[...] = own_part + cs_r[...]

    for copy in (
        cols_copy, counts_copy, *light_copies, chip_copy, *pair_copies, *pair_shares, *chip_shares,
        *chip_shares_2, check_copy, *started,
    ):
        copy.wait_send()
    for copy in out_copies:
        copy.wait()


def columns_split(start_vectors, ham_blocks, block_cols, block_counts, check_weights):
    blocks, cap, size, _ = ham_blocks.shape
    rows_n = lax.axis_size("row")
    group = 2 * blocks
    height, width = start_vectors.shape
    counts = block_counts.reshape(1, blocks)
    window = REACH + group + RIGHT_REACH
    f32, bf16 = jnp.float32, jnp.bfloat16
    heavy = cap - LIGHT
    vmem = pl.BlockSpec(memory_space=pltpu.VMEM)
    smem = pl.BlockSpec(memory_space=pltpu.SMEM)
    anywhere = pl.BlockSpec(memory_space=pl.ANY)
    filtered, check = pl.pallas_call(
        functools.partial(filter_kernel, rows_n),
        out_shape=(
            jax.ShapeDtypeStruct((height, width), f32),
            jax.ShapeDtypeStruct((1, blocks * size), f32),
        ),
        in_specs=[anywhere, anywhere, smem, smem, anywhere, anywhere, anywhere],
        out_specs=(anywhere, vmem),
        scratch_shapes=[
            pltpu.VMEM((height, width), f32),
            pltpu.VMEM((1, 2 * width), f32),
            pltpu.VMEM((height, width), f32),
            pltpu.VMEM((blocks, cap, size, size), f32),
            pltpu.VMEM((blocks, LIGHT, size, size), f32),
            pltpu.VMEM((blocks // 2, heavy, size, size), f32),
            pltpu.VMEM((blocks // 2, heavy, size, size), f32),
            pltpu.VMEM((blocks // 2, heavy, size, size), f32),
            pltpu.VMEM((heavy, size, size), f32),
            pltpu.VMEM((heavy, size, size), f32),
            pltpu.VMEM((blocks, heavy, size, size), f32),
            pltpu.SMEM((blocks, cap), jnp.int32),
            pltpu.SMEM((1, blocks), jnp.int32),
            pltpu.VMEM((group, 2 * size, cap * size), bf16),
            pltpu.VMEM((window, size, 2 * width), bf16),
            pltpu.VMEM((height, width), f32),
            pltpu.VMEM((height, width), f32),
            pltpu.VMEM((ITERS, (REACH + RIGHT_REACH) * size, width), f32),
            pltpu.VMEM((1, blocks * size), f32),
            pltpu.VMEM((1, blocks * size), f32),
            pltpu.SemaphoreType.DMA((16 + 2 * ITERS,)),
            pltpu.SemaphoreType.DMA((16 + 2 * ITERS,)),
            pltpu.SemaphoreType.DMA((5,)),
        ],
        compiler_params=pltpu.CompilerParams(
            collective_id=0, has_side_effects=True, vmem_limit_bytes=60 * 1024 * 1024
        ),
    )(start_vectors, ham_blocks, block_cols, counts, block_cols, counts, check_weights.reshape(1, -1))
    return (filtered, check.reshape(-1))


def solution(mesh):
    placed = (
        P("row", "col"),
        P(("row", "col"), None, None, None),
        P(("row", "col"), None),
        P(("row", "col")),
        P(),
    )
    devices = mesh.shape["row"] * mesh.shape["col"]
    one_heavy = devices < 64 and mesh.shape["col"] == 2 and mesh.shape["row"] >= 16 and mesh.shape["row"] % 8 == 0
    return jax.shard_map(
        columns_split if one_heavy else rows_split,
        mesh=mesh,
        in_specs=placed,
        out_specs=(P("row", "col"), P(("row", "col"))),
        check_vma=False,
    )
```

```python
import functools

import jax
import jax.numpy as jnp
from jax import lax
from jax.experimental import pallas as pl
from jax.experimental.pallas import tpu as pltpu
from jax.sharding import PartitionSpec as P

REACH = 4
RIGHT_REACH = 3
LIGHT = 3
ITERS = 3


CENTRE = 0.25
HALF_WIDTH = 1.5
HIGHEST_PRECISION = lax.Precision.HIGHEST
MESH = pl.DeviceIdType.MESH


def shifted_2(value, axis, steps):
    count = lax.axis_size(axis)
    pairs = [(source, (source + steps) % count) for source in range(count)]
    return lax.ppermute(value, axis, pairs)


def accumulate(ham_blocks, block_cols, finishes, window, window_check, base_block, total_blocks):
    block_size = ham_blocks.shape[2]
    vector_width = window.shape[1]
    results = []
    result_checks = []
    for row_index in range(ham_blocks.shape[0]):
        matrices = ham_blocks[row_index]
        columns = block_cols[row_index]

        def add_block(slot_index, carried, matrices=matrices, columns=columns):
            summed, summed_check = carried
            offset = jnp.mod(columns[slot_index] - base_block, total_blocks) * block_size
            segment = lax.dynamic_slice_in_dim(window, offset, block_size, 0)
            segment_check = lax.dynamic_slice_in_dim(window_check, offset, block_size, 0)
            matrix = lax.dynamic_index_in_dim(matrices, slot_index, 0, keepdims=False)
            summed = summed + jnp.dot(
                matrix, segment, precision=HIGHEST_PRECISION, preferred_element_type=jnp.float32
            )
            summed_check = summed_check + jnp.dot(
                matrix,
                segment_check,
                precision=HIGHEST_PRECISION,
                preferred_element_type=jnp.float32,
            )
            return (summed, summed_check)

        initial = (
            jnp.zeros((block_size, vector_width), jnp.float32),
            jnp.zeros((block_size,), jnp.float32),
        )
        summed, summed_check = lax.fori_loop(0, finishes[row_index], add_block, initial)
        results.append(summed)
        result_checks.append(summed_check)
    return (jnp.concatenate(results, 0), jnp.concatenate(result_checks, 0))


def near_window(vectors, checks, reach_devices):
    pieces = []
    piece_checks = []
    for distance in range(-reach_devices, reach_devices + 1):
        if distance == 0:
            pieces.append(vectors)
            piece_checks.append(checks)
        else:
            shifted, shifted_check = shifted_2((vectors, checks), ("row", "col"), -distance)
            pieces.append(shifted)
            piece_checks.append(shifted_check)
    return (jnp.concatenate(pieces, 0), jnp.concatenate(piece_checks, 0))


def rows_split(start_vectors, ham_blocks, block_cols, block_counts, check_weights):
    row_vectors = lax.all_to_all(start_vectors, "col", split_axis=0, concat_axis=1, tiled=True)
    checks = jnp.dot(
        row_vectors, check_weights, precision=HIGHEST_PRECISION, preferred_element_type=jnp.float32
    )
    blocks_here = ham_blocks.shape[0]
    total_blocks = lax.axis_size(("row", "col")) * blocks_here
    position = lax.axis_index(("row", "col"))
    neighbours = (REACH + blocks_here - 1) // blocks_here
    base_block = (position - neighbours) * blocks_here

    def apply_operator(vectors, vector_checks):
        window, window_check = near_window(vectors, vector_checks, neighbours)
        return accumulate(
            ham_blocks, block_cols, block_counts, window, window_check, base_block, total_blocks
        )

    previous, previous_check = (row_vectors, checks)
    image_rows, image_check = apply_operator(row_vectors, checks)
    current = (image_rows - CENTRE * row_vectors) / HALF_WIDTH
    current_check = (image_check - CENTRE * checks) / HALF_WIDTH
    for step_index in range(ITERS - 1):
        image_rows, image_check = apply_operator(current, current_check)
        following = 2.0 * (image_rows - CENTRE * current) / HALF_WIDTH - previous
        following_check = 2.0 * (image_check - CENTRE * current_check) / HALF_WIDTH - previous_check
        previous, previous_check = (current, current_check)
        current, current_check = (following, following_check)
    filtered = lax.all_to_all(current, "col", split_axis=1, concat_axis=0, tiled=True)
    return (filtered, current_check)


def split2(x):
    high = x.astype(jnp.bfloat16)
    low = (x - high.astype(jnp.float32)).astype(jnp.bfloat16)
    return high, low


def beyond(count, slot):
    return jnp.minimum(jnp.maximum(count - slot, 0), 1)


def filter_kernel(
    rows_n, v_hbm, h_ref, cols_ref, counts_ref, colsh_ref, countsh_ref, w_hbm, out_hbm, chk_ref,
    v_ref, w_ref, out_ref, hv, hr, st, es, em, ex, ec, er, colsp, countsp, a_ref, win, y1, y2,
    halo, cs_s, cs_r, send, recv, loc,
):
    r = lax.axis_index("row")
    y = lax.axis_index("col")
    right, left = lax.rem(r + 1, rows_n), lax.rem(r + rows_n - 1, rows_n)
    core = lax.rem(r, 2)
    sides = (lax.rem(r // 2, 2), lax.rem(r // 4, 2))
    blocks, cap, size, _ = hv.shape
    group = 2 * blocks
    total = rows_n * group
    heavy_slots = cap - LIGHT
    half_rows = blocks // 2
    peer = {"col": 1 - y}
    sibling = {"row": r + 1 - 2 * core}
    across = ({"row": r + 2 - 4 * sides[0]}, {"row": r + 4 - 8 * sides[1]})

    barrier = pltpu.get_barrier_semaphore()
    for target in ({"row": left}, {"row": right}, *across, peer):
        pl.semaphore_signal(barrier, inc=1, device_id=target, device_id_type=MESH)

    own_copy = pltpu.make_async_copy(h_ref, hv, loc.at[0])
    vector_copy = pltpu.make_async_copy(v_hbm, v_ref, loc.at[1])
    weight_copy = pltpu.make_async_copy(w_hbm, w_ref, loc.at[2])
    own_copy.start()
    vector_copy.start()
    weight_copy.start()
    pl.semaphore_wait(barrier, 5)

    def remote(src, dst, index, target):
        return pltpu.make_async_remote_copy(
            src_ref=src, dst_ref=dst, send_sem=send.at[index], recv_sem=recv.at[index],
            device_id=target, device_id_type=MESH,
        )

    mine_rows = [half_rows * core + side for side in sides]
    other_rows = [half_rows * core + 1 - side for side in sides]
    cols_copy = remote(colsh_ref, colsp, 0, peer)
    counts_copy = remote(countsh_ref, countsp, 1, peer)

    def light_part(part, first_row, count):
        at = pl.ds(first_row, count)
        return remote(h_ref.at[at, pl.ds(0, LIGHT)], hr.at[at], 2 + part, peer)

    lead = blocks - 1
    light_copies = (light_part(0, 0, lead), light_part(1, lead, 1))
    chip_copy = remote(st, es, 4, sibling)
    pieces = len(sides)
    piece = size // pieces
    spans = [pl.ds(k * piece, piece) for k in range(pieces)]

    def shares(rows_of, index, targets):
        copies = []
        for k in range(pieces):
            part = er.at[rows_of[k], :, spans[k]]
            copies.append(remote(part, part, index + k, targets[k]))
        return copies

    pair_copies = [
        remote(em.at[1 - sides[k], :, spans[k]], ex.at[:, spans[k]], 5 + k, across[k]) for k in range(pieces)
    ]
    cross_copies = [
        remote(ec.at[:, spans[k]], er.at[mine_rows[k], :, spans[k]], 7 + k, peer) for k in range(pieces)
    ]
    pair_shares = shares(mine_rows, 9, across)
    chip_shares = shares(mine_rows, 11, [sibling] * pieces)
    chip_shares_2 = shares(other_rows, 13, [sibling] * pieces)
    check_copy = remote(cs_s, cs_r, 15, peer)

    def halo_copies(source, step):
        own_rows = (group - REACH) * size
        to_right, to_left = [], []
        for part in range(2):
            at = part * half_rows * size
            count = half_rows * size
            to_right.append(remote(
                source.at[pl.ds(own_rows + at, count)], halo.at[step, pl.ds(at, count)],
                16 + 4 * step + part, {"row": right},
            ))
            count = min(count, RIGHT_REACH * size - at)
            to_left.append(remote(
                source.at[pl.ds(at, count)], halo.at[step, pl.ds(REACH * size + at, count)],
                18 + 4 * step + part, {"row": left},
            ))
        return to_right, to_left

    cols_copy.start()
    counts_copy.start()
    light_copies[0].start()

    def loop(count, body):
        def one(i, carry):
            body(i)
            return carry

        lax.fori_loop(0, count, one, 0, unroll=True)

    def put_window(source, src_at, dst_at, count):
        def one(i):
            at = pl.multiple_of(src_at + i * size, size)
            high, low = split2(source[pl.ds(at, size), :])
            win[dst_at + i, :, pl.ds(0, size)] = high
            win[dst_at + i, :, pl.ds(size, size)] = low

        loop(count, one)

    def put_halo(step):
        put_window(halo.at[step], 0, 0, REACH)
        put_window(halo.at[step], REACH * size, REACH + group, RIGHT_REACH)

    own_heavy = beyond(counts_ref[0, 0], LIGHT).astype(jnp.float32)

    own_copy.wait()

    def stage(i):
        st[i] = hv[half_rows * (1 - core) + i, pl.ds(LIGHT, heavy_slots)] * own_heavy

    loop(half_rows, stage)
    chip_copy.start()

    def put_slots(source, source_slot, table, half, first_row, count, slots):
        def one(i):
            i = first_row + i
            live_count = table[0, i]
            for j in slots:
                live = beyond(live_count, j).astype(jnp.float32)
                high, low = split2(source[i, j - source_slot] * live)
                a_ref[half * blocks + i, pl.ds(0, size), pl.ds(j * size, size)] = high
                a_ref[half * blocks + i, pl.ds(size, size), pl.ds(j * size, size)] = low

        loop(count, one)

    light_slots, more_slots, all_slots = range(LIGHT), range(LIGHT, cap), range(cap)
    put_slots(hv, 0, counts_ref, y, 0, blocks, light_slots)
    chip_copy.wait_recv()

    def merge(i):
        em[i] = hv[half_rows * core + i, pl.ds(LIGHT, heavy_slots)] * own_heavy + es[i]

    loop(half_rows, merge)
    for copy in pair_copies:
        copy.start()
    first = halo_copies(v_hbm, 0)
    for copy in (*first[0], *first[1]):
        copy.start()

    put_slots(hv, 0, counts_ref, y, 0, blocks, more_slots)
    vector_copy.wait()
    put_window(v_ref, 0, REACH, group)
    cols_copy.wait_recv()
    counts_copy.wait_recv()

    for k in range(pieces):
        pair_copies[k].wait_recv()
        at = spans[k]
        ec[:, at, :] = em[sides[k], :, at, :] + ex[:, at, :]
        cross_copies[k].start()

    base = r * group - REACH + total

    def tile(col):
        return win[jnp.minimum(lax.rem(col - base + 2 * total, total), win.shape[0] - 1)]

    def product(matrix, cols):
        tiles = jnp.concatenate([tile(col) for col in cols], 0)
        full = jnp.dot(matrix, tiles, preferred_element_type=jnp.float32)
        big = full[:size, :size]
        small = full[:size, size:] + full[size:, :size] + full[size:, size:]
        return big + small

    def place(half, i):
        return pl.ds(pl.multiple_of((half * blocks + i) * size, size), size)

    def image_of(half, i, slots):
        mine = y * half + (1 - y) * (1 - half)
        cols = []
        for j in slots:
            own_col, peer_col = cols_ref[i, j], colsp[i, j]
            cols.append(peer_col + mine * (own_col - peer_col))
        lanes = pl.ds(slots[0] * size, len(slots) * size)
        return product(a_ref[half * blocks + i, :, lanes], cols)

    def rows(half, source, older, target, first_row=0, count=blocks, slots=all_slots):
        def one(i):
            i = first_row + i
            image = image_of(half, i, slots)
            at = place(half, i)
            value = (image - CENTRE * source[at, :]) * (1.0 / HALF_WIDTH)
            if older is not None:
                value = 2.0 * value - older[at, :]
            target[at, :] = value

        loop(count, one)

    def share(k):
        cross_copies[k].wait_recv()
        pair_shares[k].start()
        chip_shares[k].start()

    for copy in (*first[0], *first[1]):
        copy.wait_recv()
    put_halo(0)
    rows(y, v_ref, None, y1)
    second = halo_copies(y1, 1)

    def send_halo(half, copies, part):
        @pl.when(half == 1)
        def _():
            copies[0][part].start()

        @pl.when(half == 0)
        def _():
            copies[1][part].start()

    send_halo(y, second, 0)
    send_halo(y, second, 1)
    share(0)
    share(1)
    for copy in cross_copies:
        copy.wait_send()
    light_copies[1].start()
    light_copies[0].wait_recv()
    put_slots(hr, 0, countsp, 1 - y, 0, lead, light_slots)
    rows(1 - y, v_ref, None, y1, 0, lead, light_slots)
    for k in range(pieces):
        pair_shares[k].wait_recv()
        chip_shares_2[k].start()
    for copy in (*chip_shares, *chip_shares_2):
        copy.wait_recv()
    put_slots(er, LIGHT, countsp, 1 - y, 0, blocks, more_slots)

    def add_heavy(i):
        at = place(1 - y, i)
        y1[at, :] = y1[at, :] + image_of(1 - y, i, more_slots) * (1.0 / HALF_WIDTH)

    loop(lead, add_heavy)
    send_halo(1 - y, second, 0)
    light_copies[1].wait_recv()
    put_slots(hr, 0, countsp, 1 - y, lead, 1, light_slots)
    rows(1 - y, v_ref, None, y1, lead, 1)
    send_halo(1 - y, second, 1)

    def take_halo(half, copies, step):
        @pl.when(half == 0)
        def _():
            copies[0][0].wait_recv()
            copies[0][1].wait_recv()
            put_window(halo.at[step], 0, 0, REACH)

        @pl.when(half == 1)
        def _():
            copies[1][0].wait_recv()
            copies[1][1].wait_recv()
            put_window(halo.at[step], REACH * size, REACH + group, RIGHT_REACH)

    chain = ((v_ref, None, y1), (y1, v_ref, y2), (y2, y1, out_ref))
    started = [*first, *second]
    early, late = 1 - y, y
    out_copies = []
    for step in range(1, ITERS):
        source, older, target = chain[step]
        copies = started[2 * step:]
        following = halo_copies(target, step + 1) if step < ITERS - 1 else ()
        started += following
        put_window(source, 0, REACH, group)
        for half in (early, late):
            take_halo(half, copies, step)
            if following:
                for part in range(2):
                    rows(half, source, older, target, part * half_rows, half_rows)
                    send_halo(half, following, part)
            else:
                rows(half, source, older, target)
                at = pl.ds(pl.multiple_of(half * blocks * size, size), blocks * size)
                out_copies.append(pltpu.make_async_copy(out_ref.at[at], out_hbm.at[at], loc.at[3 + len(out_copies)]))
                out_copies[-1].start()
        early, late = late, early

    weight_copy.wait()
    weights = jnp.where(y == 0, w_ref[:, :size], w_ref[:, size:])
    w_high, w_rest = split2(weights)
    w_low = (weights - w_high.astype(jnp.float32) - w_rest.astype(jnp.float32)).astype(jnp.bfloat16)
    w_parts = jnp.concatenate([w_high, w_rest, w_low, jnp.zeros((13, size), jnp.bfloat16)], 0)

    def partial(half):
        at = pl.ds(pl.multiple_of(half * blocks * size, size), blocks * size)
        total_dot = 0.0
        for part in split2(out_ref[at, :]):
            total_dot += lax.dot_general(
                w_parts, part, (((1,), (1,)), ((), ())), preferred_element_type=jnp.float32
            )
        return jnp.sum(total_dot, 0, keepdims=True)

    cs_s[...] = partial(1 - y)
    check_copy.start()
    own_part = partial(y)
    check_copy.wait_recv()
    chk_ref[...] = own_part + cs_r[...]

    for copy in (
        cols_copy, counts_copy, *light_copies, chip_copy, *pair_copies, *pair_shares, *chip_shares,
        *chip_shares_2, check_copy, *(copy for side in started for copy in side),
    ):
        copy.wait_send()
    for copy in out_copies:
        copy.wait()


def columns_split(start_vectors, ham_blocks, block_cols, block_counts, check_weights):
    blocks, cap, size, _ = ham_blocks.shape
    rows_n = lax.axis_size("row")
    group = 2 * blocks
    height, width = start_vectors.shape
    counts = block_counts.reshape(1, blocks)
    window = REACH + group + RIGHT_REACH
    f32, bf16 = jnp.float32, jnp.bfloat16
    heavy = cap - LIGHT
    vmem = pl.BlockSpec(memory_space=pltpu.VMEM)
    smem = pl.BlockSpec(memory_space=pltpu.SMEM)
    anywhere = pl.BlockSpec(memory_space=pl.ANY)
    filtered, check = pl.pallas_call(
        functools.partial(filter_kernel, rows_n),
        out_shape=(
            jax.ShapeDtypeStruct((height, width), f32),
            jax.ShapeDtypeStruct((1, blocks * size), f32),
        ),
        in_specs=[anywhere, anywhere, smem, smem, anywhere, anywhere, anywhere],
        out_specs=(anywhere, vmem),
        scratch_shapes=[
            pltpu.VMEM((height, width), f32),
            pltpu.VMEM((1, 2 * width), f32),
            pltpu.VMEM((height, width), f32),
            pltpu.VMEM((blocks, cap, size, size), f32),
            pltpu.VMEM((blocks, LIGHT, size, size), f32),
            pltpu.VMEM((blocks // 2, heavy, size, size), f32),
            pltpu.VMEM((blocks // 2, heavy, size, size), f32),
            pltpu.VMEM((blocks // 2, heavy, size, size), f32),
            pltpu.VMEM((heavy, size, size), f32),
            pltpu.VMEM((heavy, size, size), f32),
            pltpu.VMEM((blocks, heavy, size, size), f32),
            pltpu.SMEM((blocks, cap), jnp.int32),
            pltpu.SMEM((1, blocks), jnp.int32),
            pltpu.VMEM((group, 2 * size, cap * size), bf16),
            pltpu.VMEM((window, size, 2 * width), bf16),
            pltpu.VMEM((height, width), f32),
            pltpu.VMEM((height, width), f32),
            pltpu.VMEM((ITERS, (REACH + RIGHT_REACH) * size, width), f32),
            pltpu.VMEM((1, blocks * size), f32),
            pltpu.VMEM((1, blocks * size), f32),
            pltpu.SemaphoreType.DMA((16 + 4 * ITERS,)),
            pltpu.SemaphoreType.DMA((16 + 4 * ITERS,)),
            pltpu.SemaphoreType.DMA((5,)),
        ],
        compiler_params=pltpu.CompilerParams(
            collective_id=0, has_side_effects=True, vmem_limit_bytes=60 * 1024 * 1024
        ),
    )(start_vectors, ham_blocks, block_cols, counts, block_cols, counts, check_weights.reshape(1, -1))
    return (filtered, check.reshape(-1))


def solution(mesh):
    placed = (
        P("row", "col"),
        P(("row", "col"), None, None, None),
        P(("row", "col"), None),
        P(("row", "col")),
        P(),
    )
    devices = mesh.shape["row"] * mesh.shape["col"]
    one_heavy = devices < 64 and mesh.shape["col"] == 2 and mesh.shape["row"] >= 16 and mesh.shape["row"] % 8 == 0
    return jax.shard_map(
        columns_split if one_heavy else rows_split,
        mesh=mesh,
        in_specs=placed,
        out_specs=(P("row", "col"), P(("row", "col"))),
        check_vma=False,
    )
```
